512 devices in a mesh: seq: 16 (over z_lo, x), grp: 32 (over z_hi, y, core).
Axes of the slice: x: 4, y: 8, z: 8 (z_hi: 2, z_lo: 4; z = z_hi * 4 + z_lo), core: 2. Of those that a mesh axis runs over, the one named last changes fastest.
Arguments:
- compressed_vectors: bfloat16 [8192, 512], P('seq'), may hold values from -20 to 20
- starting_prototypes: float32 [8192, 512], P('grp'), may hold values from -20 to 20
- softening_scale: float32 [1], replicated, may hold values from 0.5 to 0.9
- expansion_matrix: bfloat16 [512, 32768], P(None, 'grp'), may hold values from -0.25 to 0.25
Outputs:
- decoded: bfloat16 [32, 256, 32768], P(None, 'seq', 'grp')
The draws below stay inside these ranges and needn't reach their ends.
All inputs are finite; a program needn't handle non-finite values.
Results may differ from the reference program's by a relative error of at most 0.0075.
Values may be sent and summed in bfloat16 or wider, within the bound.
A program may use at most 64 MiB of HBM per device.

```python
import jax
import jax.numpy as jnp
from jax import lax

CODE_DIMENSION = 512
CENTROIDS = 8192
ITERS = 2
CACHE_TOKENS = 8192
COLS = 32768
N_GRP = 32


def shared_source(key):
    normal_part = jnp.clip(jax.random.normal(key, (CACHE_TOKENS, CODE_DIMENSION), jnp.float32), -5.0, 5.0)
    picked = jax.random.randint(jax.random.fold_in(key, 2), (CENTROIDS,), 0, CACHE_TOKENS)
    jitter = jnp.clip(jax.random.normal(jax.random.fold_in(key, 3), (CENTROIDS, CODE_DIMENSION), jnp.float32), -5.0, 5.0)
    return (normal_part, picked, jitter)


def draw_compressed_vectors(key, part):
    normal_part, picked, jitter = shared_source(key)
    decoded_outputs = normal_part
    return decoded_outputs.astype(jnp.bfloat16)


def draw_starting_prototypes(key, part):
    normal_part, picked, jitter = shared_source(key)
    decoded_outputs = 0.6 * normal_part[picked] + 0.8 * jitter
    return decoded_outputs.astype(jnp.float32)


def block_scale(key, dims, cuts, least, largest):
    def one(position, shards_of):
        heights = jax.random.uniform(jax.random.fold_in(jax.random.fold_in(key, 6), position), (shards_of,), jnp.float32, least / len(cuts), largest / len(cuts))
        return jnp.repeat(jnp.exp(heights), dims[position] // shards_of).reshape((-1,) + (1,) * (len(dims) - position - 1))

    level = one(*cuts[0])
    for cut in cuts[1:]:
        level = level * one(*cut)
    return level


def bell_draw(stream_key, dims, scale, most, pieces=(), kind=jnp.bfloat16):
    array = jax.random.normal(stream_key, dims, jnp.float32) * scale
    if len(pieces) > 0:
        array = block_scale(stream_key, dims, pieces, -0.22, 0.18) * array
    return jnp.clip(array, min=-most, max=most).astype(kind)


def setup_inputs(seed: int = 0) -> dict:
    seeds = jax.random.split(jax.random.key(seed), 5)
    return {
        "compressed_vectors": draw_compressed_vectors(jax.random.fold_in(seeds[4], 71), 0),
        "starting_prototypes": draw_starting_prototypes(jax.random.fold_in(seeds[4], 71), 0),
        "softening_scale": jnp.clip(jax.random.uniform(seeds[2], (1,), jnp.float32, 0.5, 0.9), 0.5, 0.9),
        "expansion_matrix": bell_draw(seeds[3], (CODE_DIMENSION, COLS), CODE_DIMENSION ** -0.5, 0.25, ((1, 32),)),
    }


def reference(compressed_vectors, starting_prototypes, softening_scale, expansion_matrix):
    normalizer_amount = softening_scale[0] * jnp.sqrt(jnp.float32(CODE_DIMENSION))
    row_len = min(1024, CACHE_TOKENS)
    blocks = compressed_vectors.reshape(CACHE_TOKENS // row_len, row_len, CODE_DIMENSION)
    centers = starting_prototypes
    for iteration in range(ITERS):
        center_bf = centers.astype(jnp.bfloat16)
        squares = lax.optimization_barrier(jnp.sum(centers * centers, axis=1))

        def one_block(carry, block_rows):
            weighted, assignment_weight_total = carry
            dots = lax.dot_general(block_rows, center_bf, (((1,), (1,)), ((), ())), preferred_element_type=jnp.float32)
            logits = (2.0 * dots - squares[None, :]) / normalizer_amount
            row_max = lax.optimization_barrier(jnp.max(logits, axis=1, keepdims=True))
            expo = jnp.exp(logits - row_max)
            row_total = lax.optimization_barrier(jnp.sum(expo, axis=1, keepdims=True))
            resp = (expo / row_total).astype(jnp.bfloat16)
            weighted = weighted + lax.dot_general(resp, block_rows, (((0,), (0,)), ((), ())), preferred_element_type=jnp.float32)
            assignment_weight_total = assignment_weight_total + lax.optimization_barrier(jnp.sum(resp.astype(jnp.float32), axis=0))
            return ((weighted, assignment_weight_total), None)
        start = (jnp.zeros((CENTROIDS, CODE_DIMENSION), jnp.float32), jnp.zeros((CENTROIDS,), jnp.float32))
        (weighted, assignment_weight_total), unused = lax.scan(one_block, start, blocks)
        centers = (weighted + centers) / (assignment_weight_total[:, None] + 1.0)
    final_bf = centers.astype(jnp.bfloat16)
    decoded = jnp.dot(final_bf, expansion_matrix, preferred_element_type=jnp.float32).astype(jnp.bfloat16)
    return decoded.reshape(N_GRP, CENTROIDS // N_GRP, COLS)
```

```python
import functools

import jax
import jax.numpy as jnp
from jax import lax
from jax.experimental import pallas as pl
from jax.experimental.pallas import tpu as pltpu
from jax.sharding import PartitionSpec as P

MESH = pl.DeviceIdType.MESH
XS, ZL = 4, 4
ZH, YS, CORES = 2, 8, 2
ROWS = 16
F32, BF16 = jnp.float32, jnp.bfloat16


def ring(d, n):
    return min(d, n - d)


SEQ = sorted(
    [(z, x) for z in range(ZL) for x in range(XS) if z or x],
    key=lambda p: -(min(3, p[0]) + ring(p[1], XS)),
)
CHIPS = sorted(
    [(z, y) for z in range(ZH) for y in range(YS) if z or y],
    key=lambda p: -(4 * p[0] + ring(p[1], YS)),
)


def seq_index(z, x):
    me = lax.axis_index("seq")
    mz, mx = me // XS, me % XS
    pz = ((mz // 2 + z // 2) % 2) * 2 + (mz % 2 + z % 2) % 2
    return pz * XS + (mx + x) % XS


def grp_index(z, y, c):
    me = lax.axis_index("grp")
    mc, my, mz = me % CORES, (me // CORES) % YS, me // (CORES * YS)
    return (((mz + z) % ZH) * YS + (my + y) % YS) * CORES + (mc + c) % CORES


def split3(v):
    hi = v.astype(BF16)
    r = v - hi.astype(F32)
    mid = r.astype(BF16)
    lo = (r - mid.astype(F32)).astype(BF16)
    return hi.astype(F32), mid.astype(F32), lo.astype(F32)


def centre_tail(centres):
    half = -0.5 * jnp.sum(centres * centres, axis=1, keepdims=True)
    hi, mid, lo = split3(half)
    lane = lax.broadcasted_iota(jnp.int32, (centres.shape[0], 128), 1)
    tail = jnp.where(lane == 0, hi, jnp.where(lane == 1, mid, jnp.where(lane == 2, lo, 0.0)))
    return tail.astype(BF16)


def kernel(
    x_ref, c_ref, scale_ref, e_hbm, out_ref,
    xe, ce, e_ref, own, lse_buf, lse_src, w_src, w_buf, c_next, f_src, fin,
    e_sem, lse_s, lse_r, w_s, w_r, c_s, c_r, f_s, f_r, p_s, p_r,
):
    width = x_ref.shape[1]
    ext = width + 128
    seq = lax.axis_index("seq")

    barrier = pltpu.get_barrier_semaphore()
    peers = [{"seq": seq_index(z, x)} for z, x in SEQ]
    peers_chip = [{"grp": grp_index(z, y, 0)} for z, y in CHIPS]
    peers_other = [{"grp": grp_index(z, y, 1)} for z, y in CHIPS]
    partner = {"grp": grp_index(0, 0, 1)}
    everyone = [p for pair in zip(peers_chip, peers_other) for p in pair] + peers + [partner]
    for p in everyone:
        pl.semaphore_signal(barrier, inc=1, device_id=p, device_id_type=MESH)

    e_copy = pltpu.make_async_copy(e_hbm, e_ref, e_sem)
    e_copy.start()

    factor = 2.0 / (scale_ref[0] * jnp.sqrt(jnp.float32(width)))
    xe[:, :width] = x_ref[...]
    xe[:, width:] = jnp.ones((x_ref.shape[0], 128), BF16)
    c0 = c_ref[...]
    ce[:, :width] = c0.astype(BF16)
    ce[:, width:] = centre_tail(c0)

    sends = []

    def send(src, dst, ssem, rsem, device):
        copy = pltpu.make_async_remote_copy(
            src_ref=src, dst_ref=dst, send_sem=ssem, recv_sem=rsem,
            device_id=device, device_id_type=MESH,
        )
        copy.start()

    def drain(ref, sem):
        pltpu.make_async_copy(ref, ref, sem).wait()

    def iteration(i, centres):
        logits = factor * lax.dot_general(
            centres, xe[...], (((1,), (1,)), ((), ())), preferred_element_type=F32
        )
        top = jnp.max(logits, axis=0, keepdims=True)
        lse = top + jnp.log(jnp.sum(jnp.exp(logits - top), axis=0, keepdims=True))
        lse_src[i] = lse
        if i == 0:
            pl.semaphore_wait(barrier, len(everyone))
        slot = 0
        for a, b in zip(peers_chip, peers_other):
            for p in (a, b):
                send(lse_src.at[i], lse_buf.at[i, slot], lse_s.at[i], lse_r.at[i], p)
                slot += 1
        send(lse_src.at[i], lse_buf.at[i, slot], lse_s.at[i], lse_r.at[i], partner)
        drain(lse_buf.at[i], lse_r.at[i])
        others = lse_buf[i]
        m = jnp.maximum(jnp.max(others, axis=0), lse)
        total = jnp.sum(jnp.exp(others - m[None]), axis=0) + jnp.exp(lse - m)
        full = m + jnp.log(total)
        resp = jnp.exp(logits - full).astype(BF16)
        w = jnp.dot(resp, xe[...], preferred_element_type=F32)
        w_src[i, :, :width] = w[:, :width].astype(BF16)
        mass = w[:, width:]
        hi = mass.astype(BF16).astype(F32)
        lane = lax.broadcasted_iota(jnp.int32, mass.shape, 1)
        w_src[i, :, width:] = jnp.where(lane < 64, hi, mass - hi).astype(BF16)
        for k, (z, x) in enumerate(SEQ):
            rows = pl.ds(pl.multiple_of(seq_index(z, x) * ROWS, ROWS), ROWS)
            send(w_src.at[i, rows], w_buf.at[i, k], w_s.at[i], w_r.at[i], peers[k])
        mine = pl.ds(pl.multiple_of(seq * ROWS, ROWS), ROWS)
        acc = w_src[i, mine, :].astype(F32)
        drain(w_buf.at[i], w_r.at[i])
        for k in range(len(SEQ)):
            acc = acc + w_buf[i, k].astype(F32)
        total_mass = acc[:, width : width + 1] + acc[:, width + 64 : width + 65]
        return acc[:, :width], total_mass

    mine = pl.ds(pl.multiple_of(seq * ROWS, ROWS), ROWS)
    summed, mass = iteration(0, ce[...])
    centre = (summed + c_ref[mine, :]) / (mass + 1.0)
    own[...] = centre
    c_next[mine, :width] = centre.astype(BF16)
    c_next[mine, width:] = centre_tail(centre)
    for k in range(len(SEQ)):
        send(c_next.at[mine], c_next.at[mine], c_s, c_r, peers[k])
    drain(c_next.at[pl.ds(0, ROWS * len(SEQ))], c_r)

    summed, mass = iteration(1, c_next[...])
    fin[0, 0] = ((summed + own[...]) / (mass + 1.0)).astype(BF16)

    n = len(CHIPS)
    for k in range(n):
        send(fin.at[0, 0], fin.at[0, k + 1], f_s, f_r, peers_chip[k])
    drain(fin.at[0, pl.ds(1, n)], f_r)
    send(fin.at[0], fin.at[1], p_s, p_r, partner)
    e_copy.wait()
    me = lax.axis_index("grp")
    mc, my, mz = me % CORES, (me // CORES) % YS, me // (CORES * YS)

    def decode(half):
        rows = fin[half].reshape((n + 1) * ROWS, width)
        d = jnp.dot(rows, e_ref[...], preferred_element_type=F32).astype(BF16)
        for k in range(n + 1):
            z, y = (0, 0) if k == 0 else CHIPS[k - 1]
            g = (((mz + ZH - z) % ZH) * YS + (my + YS - y) % YS) * CORES + (mc + half) % CORES
            out_ref[g] = d[k * ROWS : (k + 1) * ROWS]

    decode(0)
    drain(fin.at[1], p_r)
    decode(1)

    for i in range(2):
        drain(lse_buf.at[i], lse_s.at[i])
        drain(w_buf.at[i], w_s.at[i])
    drain(c_next.at[pl.ds(0, ROWS * len(SEQ))], c_s)
    drain(fin.at[0, pl.ds(1, n)], f_s)
    drain(fin.at[1], p_s)


def solution(mesh):
    def per_device(x, c, scale, e):
        t, width = x.shape
        rows = c.shape[0]
        cols = e.shape[1]
        ext = width + 128
        n_grp = ZH * YS * CORES
        vmem = pl.BlockSpec(memory_space=pltpu.VMEM)
        dma = pltpu.SemaphoreType.DMA
        return pl.pallas_call(
            kernel,
            out_shape=jax.ShapeDtypeStruct((n_grp, ROWS, cols), BF16),
            in_specs=[
                vmem, vmem, pl.BlockSpec(memory_space=pltpu.SMEM), pl.BlockSpec(memory_space=pl.ANY),
            ],
            out_specs=vmem,
            scratch_shapes=[
                pltpu.VMEM((t, ext), BF16),
                pltpu.VMEM((rows, ext), BF16),
                pltpu.VMEM((width, cols), BF16),
                pltpu.VMEM((ROWS, width), F32),
                pltpu.VMEM((2, n_grp - 1, 1, t), F32),
                pltpu.VMEM((2, 1, t), F32),
                pltpu.VMEM((2, rows, ext), BF16),
                pltpu.VMEM((2, len(SEQ), ROWS, ext), BF16),
                pltpu.VMEM((rows, ext), BF16),
                pltpu.VMEM((ROWS, width), BF16),
                pltpu.VMEM((2, n_grp // 2, ROWS, width), BF16),
                dma, dma((2,)), dma((2,)), dma((2,)), dma((2,)), dma, dma, dma, dma, dma, dma,
            ],
            compiler_params=pltpu.CompilerParams(
                collective_id=0, has_side_effects=True, vmem_limit_bytes=40 * 2**20
            ),
            name="kmeans_decode",
        )(x, c, scale, e)

    placed = (P("seq", None), P("grp", None), P(), P(None, "grp"))
    return jax.shard_map(
        per_device, mesh=mesh, in_specs=placed, out_specs=P(None, "seq", "grp"), check_vma=False
    )
```

```python
import functools

import jax
import jax.numpy as jnp
from jax import lax
from jax.experimental import pallas as pl
from jax.experimental.pallas import tpu as pltpu
from jax.sharding import PartitionSpec as P

MESH = pl.DeviceIdType.MESH
XS, ZL = 4, 4
ZH, YS, CORES = 2, 8, 2
ROWS = 16
F32, BF16 = jnp.float32, jnp.bfloat16


def ring(d, n):
    return min(d, n - d)


SEQ = sorted(
    [(z, x) for z in range(ZL) for x in range(XS) if z or x],
    key=lambda p: -(min(3, p[0]) + ring(p[1], XS)),
)
CHIPS = sorted(
    [(z, y) for z in range(ZH) for y in range(YS) if z or y],
    key=lambda p: -(4 * p[0] + ring(p[1], YS)),
)


def seq_index(z, x):
    me = lax.axis_index("seq")
    mz, mx = me // XS, me % XS
    pz = ((mz // 2 + z // 2) % 2) * 2 + (mz % 2 + z % 2) % 2
    return pz * XS + (mx + x) % XS


def grp_index(z, y, c):
    me = lax.axis_index("grp")
    mc, my, mz = me % CORES, (me // CORES) % YS, me // (CORES * YS)
    return (((mz + z) % ZH) * YS + (my + y) % YS) * CORES + (mc + c) % CORES


def split3(v):
    hi = v.astype(BF16)
    r = v - hi.astype(F32)
    mid = r.astype(BF16)
    lo = (r - mid.astype(F32)).astype(BF16)
    return hi.astype(F32), mid.astype(F32), lo.astype(F32)


def centre_tail(centres):
    half = -0.5 * jnp.sum(centres * centres, axis=1, keepdims=True)
    hi, mid, lo = split3(half)
    lane = lax.broadcasted_iota(jnp.int32, (centres.shape[0], 128), 1)
    tail = jnp.where(lane == 0, hi, jnp.where(lane == 1, mid, jnp.where(lane == 2, lo, 0.0)))
    return tail.astype(BF16)


def kernel(
    x_hbm, c_hbm, scale_ref, e_hbm, out_ref,
    xe, c_ref, ce, e_ref, own, lse_buf, lse_src, w_src, w_buf, c_next, fin,
    x_sem, c_sem, e_sem, lse_s, lse_r, w_s, w_r, c_s, c_r, f_s, f_r, p_s, p_r,
):
    tokens, width = x_hbm.shape
    seq = lax.axis_index("seq")
    c_copy = pltpu.make_async_copy(c_hbm, c_ref, c_sem)
    c_copy.start()
    x_copy = pltpu.make_async_copy(x_hbm, xe.at[:, pl.ds(0, width)], x_sem)
    x_copy.start()

    barrier = pltpu.get_barrier_semaphore()
    peers = [{"seq": seq_index(z, x)} for z, x in SEQ]
    peers_chip = [{"grp": grp_index(z, y, 0)} for z, y in CHIPS]
    peers_other = [{"grp": grp_index(z, y, 1)} for z, y in CHIPS]
    partner = {"grp": grp_index(0, 0, 1)}
    everyone = [p for pair in zip(peers_chip, peers_other) for p in pair] + peers + [partner]
    for p in everyone:
        pl.semaphore_signal(barrier, inc=1, device_id=p, device_id_type=MESH)

    e_copy = pltpu.make_async_copy(e_hbm, e_ref, e_sem)
    e_copy.start()

    factor = 2.0 / (scale_ref[0] * jnp.sqrt(jnp.float32(width)))
    xe[:, width:] = jnp.ones((tokens, 128), BF16)
    c_copy.wait()
    c0 = c_ref[...]
    ce[:, :width] = c0.astype(BF16)
    ce[:, width:] = centre_tail(c0)

    x_copy.wait()
    pending = [e_copy.wait]

    def send(src, dst, ssem, rsem, device):
        copy = pltpu.make_async_remote_copy(
            src_ref=src, dst_ref=dst, send_sem=ssem, recv_sem=rsem,
            device_id=device, device_id_type=MESH,
        )
        copy.start()

    def drain(ref, sem):
        pltpu.make_async_copy(ref, ref, sem).wait()

    def iteration(i, centres):
        logits = factor * lax.dot_general(
            centres, xe[...], (((1,), (1,)), ((), ())), preferred_element_type=F32
        )
        top = jnp.max(logits, axis=0, keepdims=True)
        lse = top + jnp.log(jnp.sum(jnp.exp(logits - top), axis=0, keepdims=True))
        lse_src[i] = lse
        if i == 0:
            pl.semaphore_wait(barrier, len(everyone))
        slot = 0
        for a, b in zip(peers_chip, peers_other):
            for p in (a, b):
                send(lse_src.at[i], lse_buf.at[i, slot], lse_s.at[i], lse_r.at[i], p)
                slot += 1
        send(lse_src.at[i], lse_buf.at[i, slot], lse_s.at[i], lse_r.at[i], partner)
        pending.append(lambda: drain(lse_buf.at[i], lse_s.at[i]))
        drain(lse_buf.at[i], lse_r.at[i])
        others = lse_buf[i]
        m = jnp.maximum(jnp.max(others, axis=0), lse)
        total = jnp.sum(jnp.exp(others - m[None]), axis=0) + jnp.exp(lse - m)
        full = m + jnp.log(total)
        resp = jnp.exp(logits - full).astype(BF16)
        w = jnp.dot(resp, xe[...], preferred_element_type=F32)
        w_src[i, :, :width] = w[:, :width].astype(BF16)
        mass = w[:, width:]
        hi = mass.astype(BF16).astype(F32)
        lane = lax.broadcasted_iota(jnp.int32, mass.shape, 1)
        w_src[i, :, width:] = jnp.where(lane < 64, hi, mass - hi).astype(BF16)
        for k, (z, x) in enumerate(SEQ):
            rows = pl.ds(pl.multiple_of(seq_index(z, x) * ROWS, ROWS), ROWS)
            send(w_src.at[i, rows], w_buf.at[i, k], w_s.at[i], w_r.at[i], peers[k])
        pending.append(lambda: drain(w_buf.at[i], w_s.at[i]))
        acc = w_src[i, mine, :].astype(F32)
        drain(w_buf.at[i], w_r.at[i])
        for k in range(len(SEQ)):
            acc = acc + w_buf[i, k].astype(F32)
        total_mass = acc[:, width : width + 1] + acc[:, width + 64 : width + 65]
        return acc[:, :width], total_mass

    mine = pl.ds(pl.multiple_of(seq * ROWS, ROWS), ROWS)
    summed, mass = iteration(0, ce[...])
    centre = (summed + c_ref[mine, :]) / (mass + 1.0)
    own[...] = centre
    c_next[mine, :width] = centre.astype(BF16)
    c_next[mine, width:] = centre_tail(centre)
    for k in range(len(SEQ)):
        send(c_next.at[mine], c_next.at[mine], c_s, c_r, peers[k])
    rest = c_next.at[pl.ds(0, ROWS * len(SEQ))]
    pending.append(lambda: drain(rest, c_s))
    drain(rest, c_r)

    summed, mass = iteration(1, c_next[...])
    fin[0, 0] = ((summed + own[...]) / (mass + 1.0)).astype(BF16)

    n = len(CHIPS)
    for k in range(n):
        send(fin.at[0, 0], fin.at[0, k + 1], f_s, f_r, peers_chip[k])
    pending.append(lambda: drain(fin.at[0, pl.ds(1, n)], f_s))
    drain(fin.at[0, pl.ds(1, n)], f_r)
    send(fin.at[0], fin.at[1], p_s, p_r, partner)
    pending.append(lambda: drain(fin.at[1], p_s))
    pending.pop(0)()
    me = lax.axis_index("grp")
    mc, my, mz = me % CORES, (me // CORES) % YS, me // (CORES * YS)

    def decode(half):
        rows = fin[half].reshape((n + 1) * ROWS, width)
        d = jnp.dot(rows, e_ref[...], preferred_element_type=F32).astype(BF16)
        for k in range(n + 1):
            z, y = (0, 0) if k == 0 else CHIPS[k - 1]
            g = (((mz + ZH - z) % ZH) * YS + (my + YS - y) % YS) * CORES + (mc + half) % CORES
            out_ref[g] = d[k * ROWS : (k + 1) * ROWS]

    decode(0)
    drain(fin.at[1], p_r)
    decode(1)

    for wait in pending:
        wait()


def solution(mesh):
    def per_device(x, c, scale, e):
        t, width = x.shape
        rows = c.shape[0]
        cols = e.shape[1]
        ext = width + 128
        n_grp = ZH * YS * CORES
        vmem = pl.BlockSpec(memory_space=pltpu.VMEM)
        hbm = pl.BlockSpec(memory_space=pl.ANY)
        dma = pltpu.SemaphoreType.DMA
        return pl.pallas_call(
            kernel,
            out_shape=jax.ShapeDtypeStruct((n_grp, ROWS, cols), BF16),
            in_specs=[
                hbm, hbm, pl.BlockSpec(memory_space=pltpu.SMEM), hbm,
            ],
            out_specs=vmem,
            scratch_shapes=[
                pltpu.VMEM((t, ext), BF16),
                pltpu.VMEM((rows, width), F32),
                pltpu.VMEM((rows, ext), BF16),
                pltpu.VMEM((width, cols), BF16),
                pltpu.VMEM((ROWS, width), F32),
                pltpu.VMEM((2, n_grp - 1, 1, t), F32),
                pltpu.VMEM((2, 1, t), F32),
                pltpu.VMEM((2, rows, ext), BF16),
                pltpu.VMEM((2, len(SEQ), ROWS, ext), BF16),
                pltpu.VMEM((rows, ext), BF16),
                pltpu.VMEM((2, n_grp // 2, ROWS, width), BF16),
                dma, dma, dma, dma((2,)), dma((2,)), dma((2,)), dma((2,)), dma, dma, dma, dma, dma, dma,
            ],
            compiler_params=pltpu.CompilerParams(
                collective_id=0, has_side_effects=True, vmem_limit_bytes=56 * 2**20
            ),
            name="kmeans_decode",
        )(x, c, scale, e)

    placed = (P("seq", None), P("grp", None), P(), P(None, "grp"))
    return jax.shard_map(
        per_device, mesh=mesh, in_specs=placed, out_specs=P(None, "seq", "grp"), check_vma=False
    )
```

```python
import functools

import jax
import jax.numpy as jnp
from jax import lax
from jax.experimental import pallas as pl
from jax.experimental.pallas import tpu as pltpu
from jax.sharding import PartitionSpec as P

MESH = pl.DeviceIdType.MESH
XS, ZL = 4, 4
ZH, YS, CORES = 2, 8, 2
ROWS = 16
F32, BF16 = jnp.float32, jnp.bfloat16


def ring(d, n):
    return min(d, n - d)


SEQ = sorted(
    [(z, x) for z in range(ZL) for x in range(XS) if z or x],
    key=lambda p: -(min(3, p[0]) + ring(p[1], XS)),
)
NEAR = sorted([(0, y) for y in range(1, YS)], key=lambda p: -ring(p[1], YS))
FAR = sorted([(1, y) for y in range(YS)], key=lambda p: -ring(p[1], YS))
CHIPS = FAR + NEAR


def seq_index(z, x):
    me = lax.axis_index("seq")
    mz, mx = me // XS, me % XS
    pz = ((mz // 2 + z // 2) % 2) * 2 + (mz % 2 + z % 2) % 2
    return pz * XS + (mx + x) % XS


def grp_index(z, y, c):
    me = lax.axis_index("grp")
    mc, my, mz = me % CORES, (me // CORES) % YS, me // (CORES * YS)
    return (((mz + z) % ZH) * YS + (my + y) % YS) * CORES + (mc + c) % CORES


def kernel(
    x_hbm, c_hbm, scale_ref, e_hbm, out_ref,
    x_ref, c_ref, e_ref, own, lse_buf, lse_src, mass_buf, mass_src,
    w_src, w_buf, c_next, sq_buf, fin,
    x_sem, c_sem, e_sem,
    lse_s, lse_r, m_s, m_r, w_s, w_r, c_s, c_r, q_s, q_r, f_s, f_r, p_s, p_r,
):
    tokens, width = x_hbm.shape
    rows = c_hbm.shape[0]
    seq = lax.axis_index("seq")
    peers = [{"seq": seq_index(z, x)} for z, x in SEQ]
    peers_chip = [{"grp": grp_index(z, y, 0)} for z, y in CHIPS]
    peers_other = [{"grp": grp_index(z, y, 1)} for z, y in CHIPS]
    partner = {"grp": grp_index(0, 0, 1)}
    everyone = [p for pair in zip(peers_chip, peers_other) for p in pair] + peers + [partner]

    c_copy = pltpu.make_async_copy(c_hbm, c_ref, c_sem)
    c_copy.start()
    x_copy = pltpu.make_async_copy(x_hbm, x_ref, x_sem)
    x_copy.start()
    barrier = pltpu.get_barrier_semaphore()
    for p in everyone:
        pl.semaphore_signal(barrier, inc=1, device_id=p, device_id_type=MESH)
    e_copy = pltpu.make_async_copy(e_hbm, e_ref, e_sem)
    e_copy.start()
    pending = [e_copy.wait]

    def send(src, dst, ssem, rsem, device):
        pltpu.make_async_remote_copy(
            src_ref=src, dst_ref=dst, send_sem=ssem, recv_sem=rsem,
            device_id=device, device_id_type=MESH,
        ).start()

    def drain(ref, sem):
        pltpu.make_async_copy(ref, ref, sem).wait()

    c_copy.wait()
    c0 = c_ref[...]
    c0_bf = c0.astype(BF16)
    half0 = 0.5 * jnp.sum(c0 * c0, axis=1, keepdims=True)
    factor = 2.0 / (scale_ref[0] * jnp.sqrt(jnp.float32(width)))
    x_copy.wait()
    mine = pl.ds(pl.multiple_of(seq * ROWS, ROWS), ROWS)
    place = lax.broadcasted_iota(jnp.int32, (ROWS, rows), 1) == (
        seq * ROWS + lax.broadcasted_iota(jnp.int32, (ROWS, rows), 0)
    )

    def iteration(i, centres, half):
        dots = lax.dot_general(
            centres, x_ref[...], (((1,), (1,)), ((), ())), preferred_element_type=F32
        )
        logits = factor * (dots - half)
        top = jnp.max(logits, axis=0, keepdims=True)
        lse = top + jnp.log(jnp.sum(jnp.exp(logits - top), axis=0, keepdims=True))
        lse_src[i] = lse
        if i == 0:
            pl.semaphore_wait(barrier, len(everyone))
        slot = 0
        for a, b in zip(peers_chip, peers_other):
            for p in (a, b):
                send(lse_src.at[i], lse_buf.at[i, slot], lse_s.at[i], lse_r.at[i], p)
                slot += 1
        send(lse_src.at[i], lse_buf.at[i, slot], lse_s.at[i], lse_r.at[i], partner)
        pending.append(lambda: drain(lse_buf.at[i], lse_s.at[i]))
        drain(lse_buf.at[i], lse_r.at[i])
        others = lse_buf[i]
        m = jnp.maximum(jnp.max(others, axis=0), lse)
        total = jnp.sum(jnp.exp(others - m[None]), axis=0) + jnp.exp(lse - m)
        full = m + jnp.log(total)
        resp = jnp.exp(logits - full).astype(BF16)
        mass = lax.dot_general(
            jnp.ones((16, tokens), BF16), resp, (((1,), (1,)), ((), ())), preferred_element_type=F32
        )[0:1]
        mass_src[i] = mass
        for k in range(len(SEQ)):
            send(mass_src.at[i], mass_buf.at[i, k], m_s.at[i], m_r.at[i], peers[k])
        w = jnp.dot(resp, x_ref[...], preferred_element_type=F32)
        w_src[i] = w.astype(BF16)
        for k, (z, x) in enumerate(SEQ):
            theirs = pl.ds(pl.multiple_of(seq_index(z, x) * ROWS, ROWS), ROWS)
            send(w_src.at[i, theirs], w_buf.at[i, k], w_s.at[i], w_r.at[i], peers[k])
        pending.append(lambda: drain(mass_buf.at[i], m_s.at[i]))
        pending.append(lambda: drain(w_buf.at[i], w_s.at[i]))
        acc = w_src[i, mine, :].astype(F32)
        drain(mass_buf.at[i], m_r.at[i])
        mass = mass + jnp.sum(mass_buf[i], axis=0)
        column = jnp.sum(jnp.where(place, mass, 0.0), axis=1, keepdims=True)
        drain(w_buf.at[i], w_r.at[i])
        for k in range(len(SEQ)):
            acc = acc + w_buf[i, k].astype(F32)
        return acc, column

    summed, column = iteration(0, c0_bf, half0)
    centre = (summed + c_ref[mine, :]) / (column + 1.0)
    own[...] = centre
    c_next[mine, :] = centre.astype(BF16)
    for k in range(len(SEQ)):
        send(c_next.at[mine], c_next.at[mine], c_s, c_r, peers[k])
    half = 0.5 * jnp.sum(centre * centre, axis=1, keepdims=True)
    sq_buf[seq] = jnp.sum(jnp.where(place, half, 0.0), axis=0, keepdims=True)
    for k in range(len(SEQ)):
        send(sq_buf.at[seq], sq_buf.at[seq], q_s, q_r, peers[k])
    n_seq = len(SEQ)
    blocks = c_next.at[pl.ds(0, ROWS * n_seq)]
    lines = sq_buf.at[pl.ds(0, n_seq)]
    pending.append(lambda: drain(blocks, c_s))
    pending.append(lambda: drain(lines, q_s))
    drain(lines, q_r)
    line = jnp.sum(sq_buf[...], axis=0)
    diagonal = lax.broadcasted_iota(jnp.int32, (rows, rows), 0) == lax.broadcasted_iota(
        jnp.int32, (rows, rows), 1
    )
    half1 = jnp.sum(jnp.where(diagonal, line, 0.0), axis=1, keepdims=True)
    drain(blocks, c_r)

    summed, column = iteration(1, c_next[...], half1)
    fin[0, 0] = ((summed + own[...]) / (column + 1.0)).astype(BF16)

    near, far = len(NEAR), len(FAR)
    slots = [1 + near + k for k in range(far)] + [1 + k for k in range(near)]
    for k, slot in enumerate(slots):
        g = 1 if k < far else 0
        send(fin.at[0, 0], fin.at[0, slot], f_s.at[g], f_r.at[g], peers_chip[k])
    parts = (fin.at[0, pl.ds(1, near)], fin.at[0, pl.ds(1 + near, far)])
    halves = [[fin.at[c, pl.ds(g * (1 + near), far)] for g in range(2)] for c in range(2)]
    for g in range(2):
        pending.append(lambda g=g: drain(parts[g], f_s.at[g]))
    drain(parts[0], f_r.at[0])
    send(halves[0][0], halves[1][0], p_s.at[0], p_r.at[0], partner)
    pending.append(lambda: drain(halves[1][0], p_s.at[0]))
    drain(parts[1], f_r.at[1])
    send(halves[0][1], halves[1][1], p_s.at[1], p_r.at[1], partner)
    pending.append(lambda: drain(halves[1][1], p_s.at[1]))
    pending.pop(0)()
    me = lax.axis_index("grp")
    mc, my, mz = me % CORES, (me // CORES) % YS, me // (CORES * YS)
    chips = [(0, 0)] + NEAR + FAR

    def decode(half, first, count):
        part = fin[half, first : first + count].reshape(count * ROWS, width)
        d = jnp.dot(part, e_ref[...], preferred_element_type=F32).astype(BF16)
        for k in range(count):
            z, y = chips[first + k]
            g = (((mz + ZH - z) % ZH) * YS + (my + YS - y) % YS) * CORES + (mc + half) % CORES
            out_ref[g] = d[k * ROWS : (k + 1) * ROWS]

    decode(0, 0, 2 * far)
    drain(halves[1][0], p_r.at[0])
    decode(1, 0, far)
    drain(halves[1][1], p_r.at[1])
    decode(1, far, far)

    for wait in pending:
        wait()


def solution(mesh):
    def per_device(x, c, scale, e):
        t, width = x.shape
        rows = c.shape[0]
        cols = e.shape[1]
        n_grp = ZH * YS * CORES
        n_seq = XS * ZL
        hbm = pl.BlockSpec(memory_space=pltpu.HBM)
        dma = pltpu.SemaphoreType.DMA
        x, c, e = (pltpu.with_memory_space_constraint(v, pltpu.HBM) for v in (x, c, e))
        return pl.pallas_call(
            kernel,
            out_shape=jax.ShapeDtypeStruct((n_grp, ROWS, cols), BF16),
            in_specs=[hbm, hbm, pl.BlockSpec(memory_space=pltpu.SMEM), hbm],
            out_specs=pl.BlockSpec(memory_space=pltpu.VMEM),
            scratch_shapes=[
                pltpu.VMEM((t, width), BF16),
                pltpu.VMEM((rows, width), F32),
                pltpu.VMEM((width, cols), BF16),
                pltpu.VMEM((ROWS, width), F32),
                pltpu.VMEM((2, n_grp - 1, 1, t), F32),
                pltpu.VMEM((2, 1, t), F32),
                pltpu.VMEM((2, n_seq - 1, 1, rows), F32),
                pltpu.VMEM((2, 1, rows), F32),
                pltpu.VMEM((2, rows, width), BF16),
                pltpu.VMEM((2, n_seq - 1, ROWS, width), BF16),
                pltpu.VMEM((rows, width), BF16),
                pltpu.VMEM((n_seq, 1, rows), F32),
                pltpu.VMEM((2, n_grp // 2, ROWS, width), BF16),
                dma, dma, dma,
                dma((2,)), dma((2,)), dma((2,)), dma((2,)), dma((2,)), dma((2,)),
                dma, dma, dma, dma,
                dma((2,)), dma((2,)), dma((2,)), dma((2,)),
            ],
            compiler_params=pltpu.CompilerParams(
                collective_id=0, has_side_effects=True, vmem_limit_bytes=24 * 2**20
            ),
            name="kmeans_decode",
        )(x, c, scale, e)

    placed = (P("seq", None), P("grp", None), P(), P(None, "grp"))
    return jax.shard_map(
        per_device, mesh=mesh, in_specs=placed, out_specs=P(None, "seq", "grp"), check_vma=False
    )
```

```python
import functools

import jax
import jax.numpy as jnp
from jax import lax
from jax.experimental import pallas as pl
from jax.experimental.pallas import tpu as pltpu
from jax.sharding import PartitionSpec as P

MESH = pl.DeviceIdType.MESH
XS, ZL = 4, 4
ZH, YS, CORES = 2, 8, 2
ROWS = 16
F32, BF16 = jnp.float32, jnp.bfloat16


def ring(d, n):
    return min(d, n - d)


SEQ = sorted(
    [(z, x) for z in range(ZL) for x in range(XS) if z or x],
    key=lambda p: -(min(3, p[0]) + ring(p[1], XS)),
)
NEAR = sorted([(0, y) for y in range(1, YS)], key=lambda p: -ring(p[1], YS))
FAR = sorted([(1, y) for y in range(YS)], key=lambda p: -ring(p[1], YS))
CHIPS = FAR + NEAR


def seq_index(z, x):
    me = lax.axis_index("seq")
    mz, mx = me // XS, me % XS
    pz = ((mz // 2 + z // 2) % 2) * 2 + (mz % 2 + z % 2) % 2
    return pz * XS + (mx + x) % XS


def grp_index(z, y, c):
    me = lax.axis_index("grp")
    mc, my, mz = me % CORES, (me // CORES) % YS, me // (CORES * YS)
    return (((mz + z) % ZH) * YS + (my + y) % YS) * CORES + (mc + c) % CORES


def kernel(
    x_hbm, c_hbm, scale_ref, e_hbm, out_ref,
    x_ref, c_ref, e_ref, own, lse_buf, lse_src, mass_buf, mass_src,
    w_src, w_buf, c_next, sq_buf, fin,
    x_sem, c_sem, e_sem,
    lse_s, lse_r, m_s, m_r, w_s, w_r, c_s, c_r, q_s, q_r, f_s, f_r, p_s, p_r,
):
    tokens, width = x_hbm.shape
    rows = c_hbm.shape[0]
    seq = lax.axis_index("seq")
    peers = [{"seq": seq_index(z, x)} for z, x in SEQ]
    peers_chip = [{"grp": grp_index(z, y, 0)} for z, y in CHIPS]
    peers_other = [{"grp": grp_index(z, y, 1)} for z, y in CHIPS]
    partner = {"grp": grp_index(0, 0, 1)}
    everyone = [p for pair in zip(peers_chip, peers_other) for p in pair] + peers + [partner]

    c_copy = pltpu.make_async_copy(c_hbm, c_ref, c_sem)
    c_copy.start()
    x_copy = pltpu.make_async_copy(x_hbm, x_ref, x_sem)
    x_copy.start()
    barrier = pltpu.get_barrier_semaphore()
    for p in everyone:
        pl.semaphore_signal(barrier, inc=1, device_id=p, device_id_type=MESH)
    e_copy = pltpu.make_async_copy(e_hbm, e_ref, e_sem)
    e_copy.start()
    pending = [e_copy.wait]

    def send(src, dst, ssem, rsem, device):
        pltpu.make_async_remote_copy(
            src_ref=src, dst_ref=dst, send_sem=ssem, recv_sem=rsem,
            device_id=device, device_id_type=MESH,
        ).start()

    def drain(ref, sem):
        pltpu.make_async_copy(ref, ref, sem).wait()

    c_copy.wait()
    c0 = c_ref[...]
    half0 = 0.5 * jnp.sum(c0 * c0, axis=1, keepdims=True)
    factor = 2.0 / (scale_ref[0] * jnp.sqrt(jnp.float32(width)))
    x_copy.wait()
    cut = [slice(h * width // 2, (h + 1) * width // 2) for h in range(2)]
    mine = pl.ds(pl.multiple_of(seq * ROWS, ROWS), ROWS)
    place = lax.broadcasted_iota(jnp.int32, (ROWS, rows), 1) == (
        seq * ROWS + lax.broadcasted_iota(jnp.int32, (ROWS, rows), 0)
    )

    def iteration(i, centres, half):
        dots = sum(
            lax.dot_general(
                centres[h], x_ref[:, cut[h]], (((1,), (1,)), ((), ())), preferred_element_type=F32
            )
            for h in range(2)
        )
        logits = factor * (dots - half)
        top = jnp.max(logits, axis=0, keepdims=True)
        lse = top + jnp.log(jnp.sum(jnp.exp(logits - top), axis=0, keepdims=True))
        lse_src[i] = lse
        if i == 0:
            pl.semaphore_wait(barrier, len(everyone))
        slot = 0
        for a, b in zip(peers_chip, peers_other):
            for p in (a, b):
                send(lse_src.at[i], lse_buf.at[i, slot], lse_s.at[i], lse_r.at[i], p)
                slot += 1
        send(lse_src.at[i], lse_buf.at[i, slot], lse_s.at[i], lse_r.at[i], partner)
        pending.append(lambda: drain(lse_buf.at[i], lse_s.at[i]))
        drain(lse_buf.at[i], lse_r.at[i])
        others = lse_buf[i]
        m = jnp.maximum(jnp.max(others, axis=0), lse)
        total = jnp.sum(jnp.exp(others - m[None]), axis=0) + jnp.exp(lse - m)
        full = m + jnp.log(total)
        resp = jnp.exp(logits - full).astype(BF16)
        mass = lax.dot_general(
            jnp.ones((16, tokens), BF16), resp, (((1,), (1,)), ((), ())), preferred_element_type=F32
        )[0:1]
        mass_src[i] = mass
        for h in range(2):
            w = jnp.dot(resp, x_ref[:, cut[h]], preferred_element_type=F32)
            w_src[i, h] = w.astype(BF16)
            for k, (z, x) in enumerate(SEQ):
                theirs = pl.ds(pl.multiple_of(seq_index(z, x) * ROWS, ROWS), ROWS)
                send(w_src.at[i, h, theirs], w_buf.at[i, h, k], w_s.at[i, h], w_r.at[i, h], peers[k])
            pending.append(lambda h=h: drain(w_buf.at[i, h], w_s.at[i, h]))
            if h == 0:
                for k in range(len(SEQ)):
                    send(mass_src.at[i], mass_buf.at[i, k], m_s.at[i], m_r.at[i], peers[k])
                pending.append(lambda: drain(mass_buf.at[i], m_s.at[i]))
        drain(mass_buf.at[i], m_r.at[i])
        mass = mass + jnp.sum(mass_buf[i], axis=0)
        return jnp.sum(jnp.where(place, mass, 0.0), axis=1, keepdims=True) + 1.0

    def summed(i, h):
        acc = w_src[i, h, mine, :].astype(F32)
        drain(w_buf.at[i, h], w_r.at[i, h])
        for k in range(len(SEQ)):
            acc = acc + w_buf[i, h, k].astype(F32)
        return acc

    n_seq = len(SEQ)
    bottom = iteration(0, [c0[:, cut[h]].astype(BF16) for h in range(2)], half0)
    half = jnp.zeros((ROWS, 1), F32)
    for h in range(2):
        centre = (summed(0, h) + c_ref[mine, cut[h]]) / bottom
        own[:, cut[h]] = centre
        c_next[h, mine, :] = centre.astype(BF16)
        for k in range(n_seq):
            send(c_next.at[h, mine], c_next.at[h, mine], c_s.at[h], c_r.at[h], peers[k])
        half += 0.5 * jnp.sum(centre * centre, axis=1, keepdims=True)
    sq_buf[seq] = jnp.sum(jnp.where(place, half, 0.0), axis=0, keepdims=True)
    for k in range(n_seq):
        send(sq_buf.at[seq], sq_buf.at[seq], q_s, q_r, peers[k])
    blocks = [c_next.at[h, pl.ds(0, ROWS * n_seq)] for h in range(2)]
    lines = sq_buf.at[pl.ds(0, n_seq)]
    for h in range(2):
        pending.append(lambda h=h: drain(blocks[h], c_s.at[h]))
    pending.append(lambda: drain(lines, q_s))
    drain(blocks[0], c_r.at[0])
    drain(blocks[1], c_r.at[1])
    drain(lines, q_r)
    line = jnp.sum(sq_buf[...], axis=0)
    diagonal = lax.broadcasted_iota(jnp.int32, (rows, rows), 0) == lax.broadcasted_iota(
        jnp.int32, (rows, rows), 1
    )
    half1 = jnp.sum(jnp.where(diagonal, line, 0.0), axis=1, keepdims=True)

    bottom = iteration(1, [c_next[0], c_next[1]], half1)

    near, far = len(NEAR), len(FAR)
    slots = [1 + near + k for k in range(far)] + [1 + k for k in range(near)]
    for h in range(2):
        fin[0, 0, :, cut[h]] = ((summed(1, h) + own[:, cut[h]]) / bottom).astype(BF16)
        for k, slot in enumerate(slots):
            g = 1 if k < far else 0
            lane = pl.ds(cut[h].start, width // 2)
            send(fin.at[0, 0, :, lane], fin.at[0, slot, :, lane], f_s.at[g, h], f_r.at[g, h], peers_chip[k])
    first = (1, 1 + near)
    count = (near, far)
    parts = [
        [fin.at[0, pl.ds(first[g], count[g]), :, pl.ds(cut[h].start, width // 2)] for h in range(2)]
        for g in range(2)
    ]
    halves = [[fin.at[c, pl.ds(g * (1 + near), far)] for g in range(2)] for c in range(2)]
    for g in range(2):
        for h in range(2):
            pending.append(lambda g=g, h=h: drain(parts[g][h], f_s.at[g, h]))
    for h in range(2):
        drain(parts[0][h], f_r.at[0, h])
    send(halves[0][0], halves[1][0], p_s.at[0], p_r.at[0], partner)
    pending.append(lambda: drain(halves[1][0], p_s.at[0]))
    for h in range(2):
        drain(parts[1][h], f_r.at[1, h])
    send(halves[0][1], halves[1][1], p_s.at[1], p_r.at[1], partner)
    pending.append(lambda: drain(halves[1][1], p_s.at[1]))
    pending.pop(0)()
    me = lax.axis_index("grp")
    mc, my, mz = me % CORES, (me // CORES) % YS, me // (CORES * YS)
    chips = [(0, 0)] + NEAR + FAR

    def decode(half, first, count):
        part = fin[half, first : first + count].reshape(count * ROWS, width)
        d = jnp.dot(part, e_ref[...], preferred_element_type=F32).astype(BF16)
        for k in range(count):
            z, y = chips[first + k]
            g = (((mz + ZH - z) % ZH) * YS + (my + YS - y) % YS) * CORES + (mc + half) % CORES
            out_ref[g] = d[k * ROWS : (k + 1) * ROWS]

    decode(0, 0, 2 * far)
    drain(halves[1][0], p_r.at[0])
    decode(1, 0, far)
    drain(halves[1][1], p_r.at[1])
    decode(1, far, far)

    for wait in pending:
        wait()


def solution(mesh):
    def per_device(x, c, scale, e):
        t, width = x.shape
        rows = c.shape[0]
        cols = e.shape[1]
        n_grp = ZH * YS * CORES
        n_seq = XS * ZL
        hbm = pl.BlockSpec(memory_space=pltpu.HBM)
        dma = pltpu.SemaphoreType.DMA
        x, c, e = (pltpu.with_memory_space_constraint(v, pltpu.HBM) for v in (x, c, e))
        return pl.pallas_call(
            kernel,
            out_shape=jax.ShapeDtypeStruct((n_grp, ROWS, cols), BF16),
            in_specs=[hbm, hbm, pl.BlockSpec(memory_space=pltpu.SMEM), hbm],
            out_specs=pl.BlockSpec(memory_space=pltpu.VMEM),
            scratch_shapes=[
                pltpu.VMEM((t, width), BF16),
                pltpu.VMEM((rows, width), F32),
                pltpu.VMEM((width, cols), BF16),
                pltpu.VMEM((ROWS, width), F32),
                pltpu.VMEM((2, n_grp - 1, 1, t), F32),
                pltpu.VMEM((2, 1, t), F32),
                pltpu.VMEM((2, n_seq - 1, 1, rows), F32),
                pltpu.VMEM((2, 1, rows), F32),
                pltpu.VMEM((2, 2, rows, width // 2), BF16),
                pltpu.VMEM((2, 2, n_seq - 1, ROWS, width // 2), BF16),
                pltpu.VMEM((2, rows, width // 2), BF16),
                pltpu.VMEM((n_seq, 1, rows), F32),
                pltpu.VMEM((2, n_grp // 2, ROWS, width), BF16),
                dma, dma, dma,
                dma((2,)), dma((2,)), dma((2,)), dma((2,)), dma((2, 2)), dma((2, 2)),
                dma((2,)), dma((2,)), dma, dma,
                dma((2, 2)), dma((2, 2)), dma((2,)), dma((2,)),
            ],
            compiler_params=pltpu.CompilerParams(
                collective_id=0, has_side_effects=True, vmem_limit_bytes=24 * 2**20
            ),
            name="kmeans_decode",
        )(x, c, scale, e)

    placed = (P("seq", None), P("grp", None), P(), P(None, "grp"))
    return jax.shard_map(
        per_device, mesh=mesh, in_specs=placed, out_specs=P(None, "seq", "grp"), check_vma=False
    )
```

```python
import functools

import jax
import jax.numpy as jnp
from jax import lax
from jax.experimental import pallas as pl
from jax.experimental.pallas import tpu as pltpu
from jax.sharding import PartitionSpec as P

MESH = pl.DeviceIdType.MESH
XS, ZL = 4, 4
ZH, YS, CORES = 2, 8, 2
ROWS = 16
F32, BF16 = jnp.float32, jnp.bfloat16


def ring(d, n):
    return min(d, n - d)


SEQ = sorted(
    [(z, x) for z in range(ZL) for x in range(XS) if z or x],
    key=lambda p: -(min(3, p[0]) + ring(p[1], XS)),
)
OCTET = [p for p in SEQ if p[0] < 2]
NEAR = sorted([(0, y) for y in range(1, YS)], key=lambda p: -ring(p[1], YS))
FAR = sorted([(1, y) for y in range(YS)], key=lambda p: -ring(p[1], YS))
CHIPS = FAR + NEAR


def seq_index(z, x):
    me = lax.axis_index("seq")
    mz, mx = me // XS, me % XS
    pz = ((mz // 2 + z // 2) % 2) * 2 + (mz % 2 + z % 2) % 2
    return pz * XS + (mx + x) % XS


def grp_index(z, y, c):
    me = lax.axis_index("grp")
    mc, my, mz = me % CORES, (me // CORES) % YS, me // (CORES * YS)
    return (((mz + z) % ZH) * YS + (my + y) % YS) * CORES + (mc + c) % CORES


def kernel(
    x_hbm, c_hbm, scale_ref, e_hbm, out_ref,
    x_ref, c_ref, e_ref, own, lse_buf, lse_src, mass_buf, mass_src,
    mass_buf0, mass_src0, pair_mass, w_src, w_buf, w_src0, w_buf0, pair_src, pair_buf,
    c_next, sq_buf, fin,
    x_sem, c_sem, e_sem,
    lse_s, lse_r, m_s, m_r, w_s, w_r, m0_s, m0_r, n_s, n_r, v_s, v_r, o_s, o_r, c_s, c_r, q_s, q_r, f_s, f_r, p_s, p_r,
):
    tokens, width = x_hbm.shape
    rows = c_hbm.shape[0]
    seq = lax.axis_index("seq")
    peers = [{"seq": seq_index(z, x)} for z, x in SEQ]
    octet = [{"seq": seq_index(z, x)} for z, x in OCTET]
    across = {"seq": seq_index(2, 0)}
    peers_chip = [{"grp": grp_index(z, y, 0)} for z, y in CHIPS]
    peers_other = [{"grp": grp_index(z, y, 1)} for z, y in CHIPS]
    partner = {"grp": grp_index(0, 0, 1)}
    everyone = [p for pair in zip(peers_chip, peers_other) for p in pair] + peers + [partner]

    c_copy = pltpu.make_async_copy(c_hbm, c_ref, c_sem)
    c_copy.start()
    x_copy = pltpu.make_async_copy(x_hbm, x_ref, x_sem)
    x_copy.start()
    barrier = pltpu.get_barrier_semaphore()
    for p in everyone:
        pl.semaphore_signal(barrier, inc=1, device_id=p, device_id_type=MESH)
    e_copy = pltpu.make_async_copy(e_hbm, e_ref, e_sem)
    e_copy.start()
    pending = [e_copy.wait]

    def send(src, dst, ssem, rsem, device):
        pltpu.make_async_remote_copy(
            src_ref=src, dst_ref=dst, send_sem=ssem, recv_sem=rsem,
            device_id=device, device_id_type=MESH,
        ).start()

    def drain(ref, sem):
        pltpu.make_async_copy(ref, ref, sem).wait()

    c_copy.wait()
    c0 = c_ref[...]
    half0 = 0.5 * jnp.sum(c0 * c0, axis=1, keepdims=True)
    factor = 2.0 / (scale_ref[0] * jnp.sqrt(jnp.float32(width)))
    x_copy.wait()
    cut = [slice(h * width // 2, (h + 1) * width // 2) for h in range(2)]
    mine = pl.ds(pl.multiple_of(seq * ROWS, ROWS), ROWS)

    def softmax(i, centres, half):
        dots = sum(
            lax.dot_general(
                centres[h], x_ref[:, cut[h]], (((1,), (1,)), ((), ())), preferred_element_type=F32
            )
            for h in range(2)
        )
        logits = factor * (dots - half)
        top = jnp.max(logits, axis=0, keepdims=True)
        lse = top + jnp.log(jnp.sum(jnp.exp(logits - top), axis=0, keepdims=True))
        lse_src[i] = lse
        if i == 0:
            pl.semaphore_wait(barrier, len(everyone))
        slot = 0
        for a, b in zip(peers_chip, peers_other):
            for p in (a, b):
                send(lse_src.at[i], lse_buf.at[i, slot], lse_s.at[i], lse_r.at[i], p)
                slot += 1
        send(lse_src.at[i], lse_buf.at[i, slot], lse_s.at[i], lse_r.at[i], partner)
        pending.append(lambda: drain(lse_buf.at[i], lse_s.at[i]))
        drain(lse_buf.at[i], lse_r.at[i])
        others = lse_buf[i]
        m = jnp.maximum(jnp.max(others, axis=0), lse)
        total = jnp.sum(jnp.exp(others - m[None]), axis=0) + jnp.exp(lse - m)
        full = m + jnp.log(total)
        resp = jnp.exp(logits - full).astype(BF16)
        mass = lax.dot_general(
            jnp.ones((16, tokens), BF16), resp, (((1,), (1,)), ((), ())), preferred_element_type=F32
        )[0:1]
        return resp, mass

    n_oct = len(OCTET)
    j = seq % 8
    block = pl.ds(pl.multiple_of(j * ROWS, ROWS), ROWS)
    resp, mass = softmax(0, [c0[:, cut[h]].astype(BF16) for h in range(2)], half0)
    mass_src0[0] = mass
    for h in range(2):
        w = jnp.dot(resp, x_ref[:, cut[h]], preferred_element_type=F32)
        w_src0[h] = w.astype(BF16).reshape(2, rows // 2, width // 2)
        for k, (z, x) in enumerate(OCTET):
            theirs = pl.ds(pl.multiple_of((seq_index(z, x) % 8) * ROWS, ROWS), ROWS)
            send(w_src0.at[h, :, theirs], w_buf0.at[h, k], v_s.at[h], v_r.at[h], octet[k])
        pending.append(lambda h=h: drain(w_buf0.at[h], v_s.at[h]))
        if h == 0:
            for k in range(n_oct):
                send(mass_src0.at[0], mass_buf0.at[k], m0_s, m0_r, octet[k])
            pending.append(lambda: drain(mass_buf0, m0_s))
    for h in range(2):
        acc = w_src0[h, :, block, :].astype(F32)
        drain(w_buf0.at[h], v_r.at[h])
        for k in range(n_oct):
            acc = acc + w_buf0[h, k].astype(F32)
        pair_src[h] = acc.astype(BF16)
        send(pair_src.at[h], pair_buf.at[h], o_s.at[h], o_r.at[h], across)
        pending.append(lambda h=h: drain(pair_buf.at[h], o_s.at[h]))
        if h == 0:
            drain(mass_buf0, m0_r)
            mass = mass + jnp.sum(mass_buf0[...], axis=0)
            mass_src0[1] = mass
            send(mass_src0.at[1], pair_mass, n_s, n_r, across)
            pending.append(lambda: drain(pair_mass, n_s))
    drain(pair_mass, n_r)
    mass = mass + pair_mass[...]
    lane = lax.broadcasted_iota(jnp.int32, (ROWS, rows), 1)
    row = lax.broadcasted_iota(jnp.int32, (ROWS, rows), 0)
    spots = [lane == hi * (rows // 2) + j * ROWS + row for hi in range(2)]
    bottoms = [jnp.sum(jnp.where(s, mass, 0.0), axis=1, keepdims=True) + 1.0 for s in spots]
    halves = [jnp.zeros((ROWS, 1), F32) for _ in range(2)]
    for h in range(2):
        drain(pair_buf.at[h], o_r.at[h])
        for hi in range(2):
            start = c_ref[pl.ds(pl.multiple_of(hi * (rows // 2) + j * ROWS, ROWS), ROWS), cut[h]]
            both = pair_src[h, hi].astype(F32) + pair_buf[h, hi].astype(F32)
            centre = (both + start) / bottoms[hi]
            own[hi, :, cut[h]] = centre
            c_next[h, hi, block, :] = centre.astype(BF16)
            halves[hi] += 0.5 * jnp.sum(centre * centre, axis=1, keepdims=True)
        for k in range(n_oct):
            send(c_next.at[h, :, block], c_next.at[h, :, block], c_s.at[h], c_r.at[h], octet[k])
    sq_buf[j] = sum(
        jnp.sum(jnp.where(spots[hi], halves[hi], 0.0), axis=0, keepdims=True) for hi in range(2)
    )
    for k in range(n_oct):
        send(sq_buf.at[j], sq_buf.at[j], q_s, q_r, octet[k])
    blocks = [c_next.at[h, :, pl.ds(0, ROWS * n_oct)] for h in range(2)]
    lines = sq_buf.at[pl.ds(0, n_oct)]
    for h in range(2):
        pending.append(lambda h=h: drain(blocks[h], c_s.at[h]))
    pending.append(lambda: drain(lines, q_s))
    drain(blocks[0], c_r.at[0])
    drain(blocks[1], c_r.at[1])
    drain(lines, q_r)
    line = jnp.sum(sq_buf[...], axis=0)
    diagonal = lax.broadcasted_iota(jnp.int32, (rows, rows), 0) == lax.broadcasted_iota(
        jnp.int32, (rows, rows), 1
    )
    half1 = jnp.sum(jnp.where(diagonal, line, 0.0), axis=1, keepdims=True)

    resp, mass = softmax(1, [c_next[h].reshape(rows, width // 2) for h in range(2)], half1)
    mass_src[...] = mass
    for h in range(2):
        w = jnp.dot(resp, x_ref[:, cut[h]], preferred_element_type=F32)
        w_src[h] = w.astype(BF16)
        for k, (z, x) in enumerate(SEQ):
            theirs = pl.ds(pl.multiple_of(seq_index(z, x) * ROWS, ROWS), ROWS)
            send(w_src.at[h, theirs], w_buf.at[h, k], w_s.at[h], w_r.at[h], peers[k])
        pending.append(lambda h=h: drain(w_buf.at[h], w_s.at[h]))
        if h == 0:
            for k in range(len(SEQ)):
                send(mass_src, mass_buf.at[k], m_s, m_r, peers[k])
            pending.append(lambda: drain(mass_buf, m_s))
    drain(mass_buf, m_r)
    mass = mass + jnp.sum(mass_buf[...], axis=0)
    bottom = jnp.sum(jnp.where(lane == seq * ROWS + row, mass, 0.0), axis=1, keepdims=True) + 1.0

    def summed(h):
        acc = w_src[h, mine, :].astype(F32)
        drain(w_buf.at[h], w_r.at[h])
        for k in range(len(SEQ)):
            acc = acc + w_buf[h, k].astype(F32)
        return acc

    near, far = len(NEAR), len(FAR)
    slots = [1 + near + k for k in range(far)] + [1 + k for k in range(near)]
    for h in range(2):
        fin[0, 0, :, cut[h]] = ((summed(h) + own[seq // 8, :, cut[h]]) / bottom).astype(BF16)
        for k, slot in enumerate(slots):
            g = 1 if k < far else 0
            lane = pl.ds(cut[h].start, width // 2)
            send(fin.at[0, 0, :, lane], fin.at[0, slot, :, lane], f_s.at[g, h], f_r.at[g, h], peers_chip[k])
    first = (1, 1 + near)
    count = (near, far)
    parts = [
        [fin.at[0, pl.ds(first[g], count[g]), :, pl.ds(cut[h].start, width // 2)] for h in range(2)]
        for g in range(2)
    ]
    sides = [[fin.at[c, pl.ds(g * (1 + near), far)] for g in range(2)] for c in range(2)]
    for g in range(2):
        for h in range(2):
            pending.append(lambda g=g, h=h: drain(parts[g][h], f_s.at[g, h]))
    for h in range(2):
        drain(parts[0][h], f_r.at[0, h])
    send(sides[0][0], sides[1][0], p_s.at[0], p_r.at[0], partner)
    pending.append(lambda: drain(sides[1][0], p_s.at[0]))
    for h in range(2):
        drain(parts[1][h], f_r.at[1, h])
    send(sides[0][1], sides[1][1], p_s.at[1], p_r.at[1], partner)
    pending.append(lambda: drain(sides[1][1], p_s.at[1]))
    pending.pop(0)()
    me = lax.axis_index("grp")
    mc, my, mz = me % CORES, (me // CORES) % YS, me // (CORES * YS)
    chips = [(0, 0)] + NEAR + FAR

    def decode(half, first, count):
        part = fin[half, first : first + count].reshape(count * ROWS, width)
        d = jnp.dot(part, e_ref[...], preferred_element_type=F32).astype(BF16)
        for k in range(count):
            z, y = chips[first + k]
            g = (((mz + ZH - z) % ZH) * YS + (my + YS - y) % YS) * CORES + (mc + half) % CORES
            out_ref[g] = d[k * ROWS : (k + 1) * ROWS]

    decode(0, 0, 2 * far)
    drain(sides[1][0], p_r.at[0])
    decode(1, 0, far)
    drain(sides[1][1], p_r.at[1])
    decode(1, far, far)

    for wait in pending:
        wait()


def solution(mesh):
    def per_device(x, c, scale, e):
        t, width = x.shape
        rows = c.shape[0]
        cols = e.shape[1]
        n_grp = ZH * YS * CORES
        n_seq = XS * ZL
        n_oct = len(OCTET)
        hbm = pl.BlockSpec(memory_space=pltpu.HBM)
        dma = pltpu.SemaphoreType.DMA
        x, c, e = (pltpu.with_memory_space_constraint(v, pltpu.HBM) for v in (x, c, e))
        return pl.pallas_call(
            kernel,
            out_shape=jax.ShapeDtypeStruct((n_grp, ROWS, cols), BF16),
            in_specs=[hbm, hbm, pl.BlockSpec(memory_space=pltpu.SMEM), hbm],
            out_specs=pl.BlockSpec(memory_space=pltpu.VMEM),
            scratch_shapes=[
                pltpu.VMEM((t, width), BF16),
                pltpu.VMEM((rows, width), F32),
                pltpu.VMEM((width, cols), BF16),
                pltpu.VMEM((2, ROWS, width), F32),
                pltpu.VMEM((2, n_grp - 1, 1, t), F32),
                pltpu.VMEM((2, 1, t), F32),
                pltpu.VMEM((n_seq - 1, 1, rows), F32),
                pltpu.VMEM((1, rows), F32),
                pltpu.VMEM((n_oct, 1, rows), F32),
                pltpu.VMEM((2, 1, rows), F32),
                pltpu.VMEM((1, rows), F32),
                pltpu.VMEM((2, rows, width // 2), BF16),
                pltpu.VMEM((2, n_seq - 1, ROWS, width // 2), BF16),
                pltpu.VMEM((2, 2, rows // 2, width // 2), BF16),
                pltpu.VMEM((2, n_oct, 2, ROWS, width // 2), BF16),
                pltpu.VMEM((2, 2, ROWS, width // 2), BF16),
                pltpu.VMEM((2, 2, ROWS, width // 2), BF16),
                pltpu.VMEM((2, 2, rows // 2, width // 2), BF16),
                pltpu.VMEM((n_oct + 1, 1, rows), F32),
                pltpu.VMEM((2, n_grp // 2, ROWS, width), BF16),
                dma, dma, dma,
                dma((2,)), dma((2,)), dma, dma, dma((2,)), dma((2,)),
                dma, dma, dma, dma, dma((2,)), dma((2,)), dma((2,)), dma((2,)),
                dma((2,)), dma((2,)), dma, dma,
                dma((2, 2)), dma((2, 2)), dma((2,)), dma((2,)),
            ],
            compiler_params=pltpu.CompilerParams(
                collective_id=0, has_side_effects=True, vmem_limit_bytes=24 * 2**20
            ),
            name="kmeans_decode",
        )(x, c, scale, e)

    placed = (P("seq", None), P("grp", None), P(), P(None, "grp"))
    return jax.shard_map(
        per_device, mesh=mesh, in_specs=placed, out_specs=P(None, "seq", "grp"), check_vma=False
    )
```

```python
import functools

import jax
import jax.numpy as jnp
from jax import lax
from jax.experimental import pallas as pl
from jax.experimental.pallas import tpu as pltpu
from jax.sharding import PartitionSpec as P

MESH = pl.DeviceIdType.MESH
XS, ZL = 4, 4
ZH, YS, CORES = 2, 8, 2
ROWS = 16
F32, BF16 = jnp.float32, jnp.bfloat16


def ring(d, n):
    return min(d, n - d)


OCTET = sorted(
    [(z, x) for z in range(2) for x in range(XS) if z or x], key=lambda p: -(p[0] + ring(p[1], XS))
)
NEAR = sorted([(0, y) for y in range(1, YS)], key=lambda p: -ring(p[1], YS))
FAR = sorted([(1, y) for y in range(YS)], key=lambda p: -ring(p[1], YS))
CHIPS = FAR + NEAR


def seq_index(z, x):
    me = lax.axis_index("seq")
    mz, mx = me // XS, me % XS
    pz = ((mz // 2 + z // 2) % 2) * 2 + (mz % 2 + z % 2) % 2
    return pz * XS + (mx + x) % XS


def grp_index(z, y, c):
    me = lax.axis_index("grp")
    mc, my, mz = me % CORES, (me // CORES) % YS, me // (CORES * YS)
    return (((mz + z) % ZH) * YS + (my + y) % YS) * CORES + (mc + c) % CORES


def kernel(
    x_hbm, c_hbm, scale_ref, e_hbm, out_ref,
    x_ref, c_ref, e_ref, own, lse_buf, lse_src, mass_buf, mass_src, pair_mass,
    w_src, w_buf, pair_src, pair_buf, last_src, last_buf, c_src, c_next, sq_src, sq_buf, fin,
    x_sem, c_sem, e_sem,
    lse_s, lse_r, m_s, m_r, n_s, n_r, w_s, w_r, o_s, o_r, l_s, l_r,
    c_s, c_r, q_s, q_r, f_s, f_r, p_s, p_r,
):
    tokens, width = x_hbm.shape
    rows = c_hbm.shape[0]
    seq = lax.axis_index("seq")
    partner_group = grp_index(0, 0, 1)
    octet = [{"seq": seq_index(z, x), "grp": partner_group} for z, x in OCTET] + [{"grp": partner_group}]
    octet_index = [seq_index(z, x) % 8 for z, x in OCTET] + [seq % 8]
    across = {"seq": seq_index(2, 0)}
    peers_chip = [{"grp": grp_index(z, y, 0)} for z, y in CHIPS]
    peers_other = [{"grp": grp_index(z, y, 1)} for z, y in CHIPS]
    partner = {"grp": partner_group}
    everyone = [p for pair in zip(peers_chip, peers_other) for p in pair] + octet + [across]

    c_copy = pltpu.make_async_copy(c_hbm, c_ref, c_sem)
    c_copy.start()
    x_copy = pltpu.make_async_copy(x_hbm, x_ref, x_sem)
    x_copy.start()
    barrier = pltpu.get_barrier_semaphore()
    for p in everyone:
        pl.semaphore_signal(barrier, inc=1, device_id=p, device_id_type=MESH)
    e_copy = pltpu.make_async_copy(e_hbm, e_ref, e_sem)
    e_copy.start()
    pending = [e_copy.wait]

    def send(src, dst, ssem, rsem, device):
        pltpu.make_async_remote_copy(
            src_ref=src, dst_ref=dst, send_sem=ssem, recv_sem=rsem,
            device_id=device, device_id_type=MESH,
        ).start()

    def drain(ref, sem):
        pltpu.make_async_copy(ref, ref, sem).wait()

    c_copy.wait()
    c0 = c_ref[...]
    half0 = 0.5 * jnp.sum(c0 * c0, axis=1, keepdims=True)
    factor = 2.0 / (scale_ref[0] * jnp.sqrt(jnp.float32(width)))
    x_copy.wait()
    cut = [slice(h * width // 2, (h + 1) * width // 2) for h in range(2)]

    def softmax(i, centres, half):
        dots = sum(
            lax.dot_general(
                centres[h], x_ref[:, cut[h]], (((1,), (1,)), ((), ())), preferred_element_type=F32
            )
            for h in range(2)
        )
        logits = factor * (dots - half)
        top = jnp.max(logits, axis=0, keepdims=True)
        lse = top + jnp.log(jnp.sum(jnp.exp(logits - top), axis=0, keepdims=True))
        lse_src[i] = lse
        if i == 0:
            pl.semaphore_wait(barrier, len(everyone))
        slot = 0
        for a, b in zip(peers_chip, peers_other):
            for p in (a, b):
                send(lse_src.at[i], lse_buf.at[i, slot], lse_s.at[i], lse_r.at[i], p)
                slot += 1
        send(lse_src.at[i], lse_buf.at[i, slot], lse_s.at[i], lse_r.at[i], partner)
        pending.append(lambda: drain(lse_buf.at[i], lse_s.at[i]))
        drain(lse_buf.at[i], lse_r.at[i])
        others = lse_buf[i]
        m = jnp.maximum(jnp.max(others, axis=0), lse)
        total = jnp.sum(jnp.exp(others - m[None]), axis=0) + jnp.exp(lse - m)
        full = m + jnp.log(total)
        resp = jnp.exp(logits - full).astype(BF16)
        mass = lax.dot_general(
            jnp.ones((16, tokens), BF16), resp, (((1,), (1,)), ((), ())), preferred_element_type=F32
        )[0:1]
        return resp, mass

    n_oct = len(octet)
    j, hi = seq % 8, seq // 8
    lane = lax.broadcasted_iota(jnp.int32, (ROWS, rows), 1)
    row = lax.broadcasted_iota(jnp.int32, (ROWS, rows), 0)
    spots = [lane == q * (rows // 2) + j * ROWS + row for q in range(2)]

    def scatter(i, resp, mass):
        mass_src[i, 0] = mass
        for h in range(2):
            w = jnp.dot(resp, x_ref[:, cut[h]], preferred_element_type=F32)
            w_src[i, h] = w.astype(BF16).reshape(2, rows // 2, width // 2)
            if i == 0:
                mine = pl.ds(pl.multiple_of(j * ROWS, ROWS), ROWS)
                w_src[0, h, hi, mine, :] = (
                    w_src[0, h, hi, mine, :].astype(F32)
                    + c_ref[pl.ds(pl.multiple_of(seq * ROWS, ROWS), ROWS), cut[h]]
                ).astype(BF16)
            for k in range(n_oct):
                theirs = pl.ds(pl.multiple_of(octet_index[k] * ROWS, ROWS), ROWS)
                send(w_src.at[i, h, :, theirs], w_buf.at[i, h, k], w_s.at[i, h], w_r.at[i, h], octet[k])
            pending.append(lambda h=h: drain(w_buf.at[i, h], w_s.at[i, h]))
            if h == 0:
                for k in range(n_oct):
                    send(mass_src.at[i, 0], mass_buf.at[i, k], m_s.at[i], m_r.at[i], octet[k])
                pending.append(lambda: drain(mass_buf.at[i], m_s.at[i]))

    def partial(i, h, side):
        acc = w_buf[i, h, 0, side].astype(F32)
        for k in range(1, n_oct):
            acc = acc + w_buf[i, h, k, side].astype(F32)
        return acc

    def pair_up_mass(i):
        drain(mass_buf.at[i], m_r.at[i])
        mass = jnp.sum(mass_buf[i], axis=0)
        mass_src[i, 1] = mass
        send(mass_src.at[i, 1], pair_mass.at[i], n_s.at[i], n_r.at[i], across)
        pending.append(lambda: drain(pair_mass.at[i], n_s.at[i]))
        return mass

    scatter(0, *softmax(0, [c0[:, cut[h]].astype(BF16) for h in range(2)], half0))
    for h in range(2):
        drain(w_buf.at[0, h], w_r.at[0, h])
        for q in range(2):
            pair_src[h, q] = partial(0, h, q).astype(BF16)
        send(pair_src.at[h], pair_buf.at[h], o_s.at[h], o_r.at[h], across)
        pending.append(lambda h=h: drain(pair_buf.at[h], o_s.at[h]))
        if h == 0:
            mass = pair_up_mass(0)
    drain(pair_mass.at[0], n_r.at[0])
    mass = mass + pair_mass[0]
    bottoms = [jnp.sum(jnp.where(s, mass, 0.0), axis=1, keepdims=True) + 1.0 for s in spots]
    halves = [jnp.zeros((ROWS, 1), F32) for _ in range(2)]
    block = pl.ds(pl.multiple_of(j * ROWS, ROWS), ROWS)
    for h in range(2):
        drain(pair_buf.at[h], o_r.at[h])
        for q in range(2):
            both = pair_src[h, q].astype(F32) + pair_buf[h, q].astype(F32)
            centre = both / bottoms[q]
            own[q, :, cut[h]] = centre
            c_src[h, q] = centre.astype(BF16)
            halves[q] += 0.5 * jnp.sum(centre * centre, axis=1, keepdims=True)
        for k in range(n_oct):
            send(c_src.at[h], c_next.at[h, :, block], c_s.at[h], c_r.at[h], octet[k])
        pending.append(lambda h=h: drain(c_next.at[h], c_s.at[h]))
    sq_src[...] = sum(
        jnp.sum(jnp.where(spots[q], halves[q], 0.0), axis=0, keepdims=True) for q in range(2)
    )
    for k in range(n_oct):
        send(sq_src, sq_buf.at[j], q_s, q_r, octet[k])
    pending.append(lambda: drain(sq_buf, q_s))
    drain(c_next.at[0], c_r.at[0])
    drain(c_next.at[1], c_r.at[1])
    drain(sq_buf, q_r)
    line = jnp.sum(sq_buf[...], axis=0)
    diagonal = lax.broadcasted_iota(jnp.int32, (rows, rows), 0) == lax.broadcasted_iota(
        jnp.int32, (rows, rows), 1
    )
    half1 = jnp.sum(jnp.where(diagonal, line, 0.0), axis=1, keepdims=True)

    scatter(1, *softmax(1, [c_next[h].reshape(rows, width // 2) for h in range(2)], half1))
    kept = []
    for h in range(2):
        drain(w_buf.at[1, h], w_r.at[1, h])
        last_src[h] = partial(1, h, 1 - hi).astype(BF16)
        send(last_src.at[h], last_buf.at[h], l_s.at[h], l_r.at[h], across)
        pending.append(lambda h=h: drain(last_buf.at[h], l_s.at[h]))
        kept.append(partial(1, h, hi))
        if h == 0:
            mass = pair_up_mass(1)
    drain(pair_mass.at[1], n_r.at[1])
    mass = mass + pair_mass[1]
    bottom = jnp.sum(jnp.where(lane == seq * ROWS + row, mass, 0.0), axis=1, keepdims=True) + 1.0

    def summed(h):
        drain(last_buf.at[h], l_r.at[h])
        return kept[h] + last_buf[h].astype(F32)

    near, far = len(NEAR), len(FAR)
    slots = [1 + near + k for k in range(far)] + [1 + k for k in range(near)]
    first, count = (1, 1 + near), (near, far)
    for h in range(2):
        fin[1, 0, :, cut[h]] = ((summed(h) + own[hi, :, cut[h]]) / bottom).astype(BF16)
        for k, slot in enumerate(slots):
            g = 1 if k < far else 0
            lanes = pl.ds(cut[h].start, width // 2)
            send(fin.at[1, 0, :, lanes], fin.at[0, slot, :, lanes], f_s.at[g, h], f_r.at[g, h], peers_other[k])
    send(fin.at[1, 0], fin.at[0, 0], p_s.at[0], p_r.at[0], partner)
    pending.append(lambda: drain(fin.at[0, 0], p_s.at[0]))
    parts = [
        [fin.at[0, pl.ds(first[g], count[g]), :, pl.ds(cut[h].start, width // 2)] for h in range(2)]
        for g in range(2)
    ]
    sides = [[fin.at[c, pl.ds(first[g], count[g])] for g in range(2)] for c in range(2)]
    for g in range(2):
        for h in range(2):
            pending.append(lambda g=g, h=h: drain(parts[g][h], f_s.at[g, h]))
    for g in range(2):
        for h in range(2):
            drain(parts[g][h], f_r.at[g, h])
        send(sides[0][g], sides[1][g], p_s.at[g + 1], p_r.at[g + 1], partner)
        pending.append(lambda g=g: drain(sides[1][g], p_s.at[g + 1]))
    pending.pop(0)()
    drain(fin.at[0, 0], p_r.at[0])
    me = lax.axis_index("grp")
    mc, my, mz = me % CORES, (me // CORES) % YS, me // (CORES * YS)
    chips = [(0, 0)] + NEAR + FAR

    def decode(half, first, count):
        part = fin[half, first : first + count].reshape(count * ROWS, width)
        d = jnp.dot(part, e_ref[...], preferred_element_type=F32).astype(BF16)
        for k in range(count):
            z, y = chips[first + k]
            g = (((mz + ZH - z) % ZH) * YS + (my + YS - y) % YS) * CORES + (mc + half) % CORES
            out_ref[g] = d[k * ROWS : (k + 1) * ROWS]

    decode(0, 0, 2 * far)
    drain(sides[1][0], p_r.at[1])
    decode(1, 0, far)
    drain(sides[1][1], p_r.at[2])
    decode(1, far, far)

    for wait in pending:
        wait()


def solution(mesh):
    def per_device(x, c, scale, e):
        t, width = x.shape
        rows = c.shape[0]
        cols = e.shape[1]
        n_grp = ZH * YS * CORES
        n_oct = len(OCTET) + 1
        hbm = pl.BlockSpec(memory_space=pltpu.HBM)
        dma = pltpu.SemaphoreType.DMA
        x, c, e = (pltpu.with_memory_space_constraint(v, pltpu.HBM) for v in (x, c, e))
        return pl.pallas_call(
            kernel,
            out_shape=jax.ShapeDtypeStruct((n_grp, ROWS, cols), BF16),
            in_specs=[hbm, hbm, pl.BlockSpec(memory_space=pltpu.SMEM), hbm],
            out_specs=pl.BlockSpec(memory_space=pltpu.VMEM),
            scratch_shapes=[
                pltpu.VMEM((t, width), BF16),
                pltpu.VMEM((rows, width), F32),
                pltpu.VMEM((width, cols), BF16),
                pltpu.VMEM((2, ROWS, width), F32),
                pltpu.VMEM((2, n_grp - 1, 1, t), F32),
                pltpu.VMEM((2, 1, t), F32),
                pltpu.VMEM((2, n_oct, 1, rows), F32),
                pltpu.VMEM((2, 2, 1, rows), F32),
                pltpu.VMEM((2, 1, rows), F32),
                pltpu.VMEM((2, 2, 2, rows // 2, width // 2), BF16),
                pltpu.VMEM((2, 2, n_oct, 2, ROWS, width // 2), BF16),
                pltpu.VMEM((2, 2, ROWS, width // 2), BF16),
                pltpu.VMEM((2, 2, ROWS, width // 2), BF16),
                pltpu.VMEM((2, ROWS, width // 2), BF16),
                pltpu.VMEM((2, ROWS, width // 2), BF16),
                pltpu.VMEM((2, 2, ROWS, width // 2), BF16),
                pltpu.VMEM((2, 2, rows // 2, width // 2), BF16),
                pltpu.VMEM((1, rows), F32),
                pltpu.VMEM((n_oct, 1, rows), F32),
                pltpu.VMEM((2, n_grp // 2, ROWS, width), BF16),
                dma, dma, dma,
                dma((2,)), dma((2,)), dma((2,)), dma((2,)), dma((2,)), dma((2,)),
                dma((2, 2)), dma((2, 2)), dma((2,)), dma((2,)), dma((2,)), dma((2,)),
                dma((2,)), dma((2,)), dma, dma,
                dma((2, 2)), dma((2, 2)), dma((3,)), dma((3,)),
            ],
            compiler_params=pltpu.CompilerParams(
                collective_id=0, has_side_effects=True, vmem_limit_bytes=24 * 2**20
            ),
            name="kmeans_decode",
        )(x, c, scale, e)

    placed = (P("seq", None), P("grp", None), P(), P(None, "grp"))
    return jax.shard_map(
        per_device, mesh=mesh, in_specs=placed, out_specs=P(None, "seq", "grp"), check_vma=False
    )
```

```python
import functools

import jax
import jax.numpy as jnp
from jax import lax
from jax.experimental import pallas as pl
from jax.experimental.pallas import tpu as pltpu
from jax.sharding import PartitionSpec as P

MESH = pl.DeviceIdType.MESH
XS, ZL = 4, 4
ZH, YS, CORES = 2, 8, 2
ROWS = 16
F32, BF16 = jnp.float32, jnp.bfloat16
PIECES = (2, 2)


def ring(d, n):
    return min(d, n - d)


OCTET = sorted(
    [(z, x) for z in range(2) for x in range(XS) if z or x], key=lambda p: -(p[0] + ring(p[1], XS))
)
NEAR = sorted([(0, y) for y in range(1, YS)], key=lambda p: -ring(p[1], YS))
FAR = sorted([(1, y) for y in range(YS)], key=lambda p: -ring(p[1], YS))
CHIPS = FAR + NEAR


def seq_index(z, x):
    me = lax.axis_index("seq")
    mz, mx = me // XS, me % XS
    pz = ((mz // 2 + z // 2) % 2) * 2 + (mz % 2 + z % 2) % 2
    return pz * XS + (mx + x) % XS


def grp_index(z, y, c):
    me = lax.axis_index("grp")
    mc, my, mz = me % CORES, (me // CORES) % YS, me // (CORES * YS)
    return (((mz + z) % ZH) * YS + (my + y) % YS) * CORES + (mc + c) % CORES


def kernel(
    x_hbm, c_hbm, scale_ref, e_hbm, out_ref,
    x_ref, c_ref, e_ref, own, theirs_c, lse_buf, lse_src, mass_buf, mass_src, pair_mass,
    w_src0, w_src1, w_buf0, w_buf1, pair_src, pair_buf, last_src, last_buf, c_src, c_next, sq_src, sq_buf, fin,
    x_sem, c_sem, e_sem, a_s, a_r,
    lse_s, lse_r, m_s, m_r, n_s, n_r, w_s, w_r, o_s, o_r, l_s, l_r,
    c_s, c_r, q_s, q_r, f_s, f_r, p_s, p_r, h_s, h_r,
):
    tokens, width = x_hbm.shape
    rows = c_hbm.shape[0]
    w_src, w_buf = (w_src0, w_src1), (w_buf0, w_buf1)
    seq = lax.axis_index("seq")
    partner_group = grp_index(0, 0, 1)
    octet = [{"seq": seq_index(z, x), "grp": partner_group} for z, x in OCTET] + [{"grp": partner_group}]
    octet_index = [seq_index(z, x) % 8 for z, x in OCTET] + [seq % 8]
    across = {"seq": seq_index(2, 0)}
    peers_chip = [{"grp": grp_index(z, y, 0)} for z, y in CHIPS]
    peers_other = [{"grp": grp_index(z, y, 1)} for z, y in CHIPS]
    partner = {"grp": partner_group}
    everyone = [p for pair in zip(peers_chip, peers_other) for p in pair] + octet + [across]

    c_copy = pltpu.make_async_copy(c_hbm, c_ref, c_sem)
    c_copy.start()
    x_copy = pltpu.make_async_copy(x_hbm, x_ref, x_sem)
    x_copy.start()
    barrier = pltpu.get_barrier_semaphore()
    for p in everyone:
        pl.semaphore_signal(barrier, inc=1, device_id=p, device_id_type=MESH)
    e_copy = pltpu.make_async_copy(e_hbm, e_ref, e_sem)
    e_copy.start()
    pending = [e_copy.wait]

    def send(src, dst, ssem, rsem, device):
        pltpu.make_async_remote_copy(
            src_ref=src, dst_ref=dst, send_sem=ssem, recv_sem=rsem,
            device_id=device, device_id_type=MESH,
        ).start()

    def drain(ref, sem):
        pltpu.make_async_copy(ref, ref, sem).wait()

    c_copy.wait()
    c0 = c_ref[...]
    half0 = 0.5 * jnp.sum(c0 * c0, axis=1, keepdims=True)
    factor = 2.0 / (scale_ref[0] * jnp.sqrt(jnp.float32(width)))
    x_copy.wait()
    size = [width // n for n in PIECES]
    cuts = [[slice(h * size[i], (h + 1) * size[i]) for h in range(n)] for i, n in enumerate(PIECES)]

    def softmax(i, centres, half):
        dots = sum(
            lax.dot_general(
                centres[h], x_ref[:, cuts[0][h]], (((1,), (1,)), ((), ())), preferred_element_type=F32
            )
            for h in range(PIECES[0])
        )
        logits = factor * (dots - half)
        top = jnp.max(logits, axis=0, keepdims=True)
        lse = top + jnp.log(jnp.sum(jnp.exp(logits - top), axis=0, keepdims=True))
        lse_src[i] = lse
        if i == 0:
            pl.semaphore_wait(barrier, len(everyone))
        slot = 0
        for a, b in zip(peers_chip, peers_other):
            for p in (a, b):
                send(lse_src.at[i], lse_buf.at[i, slot], lse_s.at[i], lse_r.at[i], p)
                slot += 1
        send(lse_src.at[i], lse_buf.at[i, slot], lse_s.at[i], lse_r.at[i], partner)
        pending.append(lambda: drain(lse_buf.at[i], lse_s.at[i]))
        if i == 0:
            for q in range(2):
                start = pl.ds(pl.multiple_of(q * (rows // 2) + (seq % 8) * ROWS, ROWS), ROWS)
                send(c_ref.at[start], theirs_c.at[q], a_s, a_r, partner)
            pending.append(lambda: drain(theirs_c, a_s))
        drain(lse_buf.at[i], lse_r.at[i])
        others = lse_buf[i]
        m = jnp.maximum(jnp.max(others, axis=0), lse)
        total = jnp.sum(jnp.exp(others - m[None]), axis=0) + jnp.exp(lse - m)
        full = m + jnp.log(total)
        resp = jnp.exp(logits - full).astype(BF16)
        return resp

    n_oct = len(octet)
    j, hi = seq % 8, seq // 8
    lane = lax.broadcasted_iota(jnp.int32, (ROWS, rows), 1)
    row = lax.broadcasted_iota(jnp.int32, (ROWS, rows), 0)
    spots = [lane == q * (rows // 2) + j * ROWS + row for q in range(2)]

    def scatter(i, resp):
        for h, cut in enumerate(cuts[i]):
            w = jnp.dot(resp, x_ref[:, cut], preferred_element_type=F32)
            w_src[i][h] = w.astype(BF16).reshape(2, rows // 2, size[i])
            for k in range(n_oct):
                theirs = pl.ds(pl.multiple_of(octet_index[k] * ROWS, ROWS), ROWS)
                send(w_src[i].at[h, :, theirs], w_buf[i].at[h, k], w_s.at[i, h], w_r.at[i, h], octet[k])
            pending.append(lambda h=h: drain(w_buf[i].at[h], w_s.at[i, h]))
            if h == 0:
                mass = lax.dot_general(
                    jnp.ones((16, tokens), BF16), resp, (((1,), (1,)), ((), ())),
                    preferred_element_type=F32,
                )
                mass_src[i, 0] = mass[0:1]
                for k in range(n_oct):
                    send(mass_src.at[i, 0], mass_buf.at[i, k], m_s.at[i], m_r.at[i], octet[k])
                pending.append(lambda: drain(mass_buf.at[i], m_s.at[i]))

    def partial(i, h, side):
        acc = w_buf[i][h, 0, side].astype(F32)
        for k in range(1, n_oct):
            acc = acc + w_buf[i][h, k, side].astype(F32)
        return acc

    def pair_up_mass(i):
        drain(mass_buf.at[i], m_r.at[i])
        mass = jnp.sum(mass_buf[i], axis=0)
        mass_src[i, 1] = mass
        send(mass_src.at[i, 1], pair_mass.at[i], n_s.at[i], n_r.at[i], across)
        pending.append(lambda: drain(pair_mass.at[i], n_s.at[i]))
        return mass

    scatter(0, softmax(0, [c0[:, cut].astype(BF16) for cut in cuts[0]], half0))
    for h in range(PIECES[0]):
        drain(w_buf[0].at[h], w_r.at[0, h])
        for q in range(2):
            pair_src[h, q] = partial(0, h, q).astype(BF16)
        send(pair_src.at[h], pair_buf.at[h], o_s.at[h], o_r.at[h], across)
        pending.append(lambda h=h: drain(pair_buf.at[h], o_s.at[h]))
        if h == 0:
            mass = pair_up_mass(0)
    drain(pair_mass.at[0], n_r.at[0])
    mass = mass + pair_mass[0]
    bottoms = [jnp.sum(jnp.where(s, mass, 0.0), axis=1, keepdims=True) + 1.0 for s in spots]
    halves = [jnp.zeros((ROWS, 1), F32) for _ in range(2)]
    block = pl.ds(pl.multiple_of(j * ROWS, ROWS), ROWS)
    drain(theirs_c, a_r)
    for h, cut in enumerate(cuts[0]):
        drain(pair_buf.at[h], o_r.at[h])
        for q in range(2):
            both = pair_src[h, q].astype(F32) + pair_buf[h, q].astype(F32)
            centre = (both + theirs_c[q, :, cut]) / bottoms[q]
            own[q, :, cut] = centre
            c_src[h, q] = centre.astype(BF16)
            halves[q] += 0.5 * jnp.sum(centre * centre, axis=1, keepdims=True)
        for k in range(n_oct):
            send(c_src.at[h], c_next.at[h, :, block], c_s.at[h], c_r.at[h], octet[k])
        pending.append(lambda h=h: drain(c_next.at[h], c_s.at[h]))
    sq_src[...] = sum(
        jnp.sum(jnp.where(spots[q], halves[q], 0.0), axis=0, keepdims=True) for q in range(2)
    )
    for k in range(n_oct):
        send(sq_src, sq_buf.at[j], q_s, q_r, octet[k])
    pending.append(lambda: drain(sq_buf, q_s))
    for h in range(PIECES[0]):
        drain(c_next.at[h], c_r.at[h])
    drain(sq_buf, q_r)
    line = jnp.sum(sq_buf[...], axis=0)
    diagonal = lax.broadcasted_iota(jnp.int32, (rows, rows), 0) == lax.broadcasted_iota(
        jnp.int32, (rows, rows), 1
    )
    half1 = jnp.sum(jnp.where(diagonal, line, 0.0), axis=1, keepdims=True)

    scatter(1, softmax(1, [c_next[h].reshape(rows, size[0]) for h in range(PIECES[0])], half1))
    kept = []
    for h in range(PIECES[1]):
        drain(w_buf[1].at[h], w_r.at[1, h])
        last_src[h] = partial(1, h, 1 - hi).astype(BF16)
        send(last_src.at[h], last_buf.at[h], l_s.at[h], l_r.at[h], across)
        pending.append(lambda h=h: drain(last_buf.at[h], l_s.at[h]))
        kept.append(partial(1, h, hi))
        if h == 0:
            mass = pair_up_mass(1)
    drain(pair_mass.at[1], n_r.at[1])
    mass = mass + pair_mass[1]
    bottom = jnp.sum(jnp.where(lane == seq * ROWS + row, mass, 0.0), axis=1, keepdims=True) + 1.0

    def summed(h):
        drain(last_buf.at[h], l_r.at[h])
        return kept[h] + last_buf[h].astype(F32)

    near, far = len(NEAR), len(FAR)
    slots = [1 + near + k for k in range(far)] + [1 + k for k in range(near)]
    first, count = (1, 1 + near), (near, far)
    for h, cut in enumerate(cuts[1]):
        fin[1, 0, :, cut] = ((summed(h) + own[hi, :, cut]) / bottom).astype(BF16)
        lanes = pl.ds(cut.start, size[1])
        for k, slot in enumerate(slots):
            g = 1 if k < far else 0
            send(fin.at[1, 0, :, lanes], fin.at[0, slot, :, lanes], f_s.at[g, h], f_r.at[g, h], peers_other[k])
    send(fin.at[1, 0], fin.at[0, 0], p_s, p_r, partner)
    pending.append(lambda: drain(fin.at[0, 0], p_s))

    def part(c, g, h):
        return fin.at[c, pl.ds(first[g], count[g]), :, pl.ds(cuts[1][h].start, size[1])]

    for g in range(2):
        for h in range(PIECES[1]):
            pending.append(lambda g=g, h=h: drain(part(0, g, h), f_s.at[g, h]))
            drain(part(0, g, h), f_r.at[g, h])
            send(part(0, g, h), part(1, g, h), h_s.at[g, h], h_r.at[g, h], partner)
            pending.append(lambda g=g, h=h: drain(part(1, g, h), h_s.at[g, h]))
    pending.pop(0)()
    drain(fin.at[0, 0], p_r)
    me = lax.axis_index("grp")
    mc, my, mz = me % CORES, (me // CORES) % YS, me // (CORES * YS)
    chips = [(0, 0)] + NEAR + FAR

    def decode(half, first, count):
        part = fin[half, first : first + count].reshape(count * ROWS, width)
        d = jnp.dot(part, e_ref[...], preferred_element_type=F32).astype(BF16)
        for k in range(count):
            z, y = chips[first + k]
            g = (((mz + ZH - z) % ZH) * YS + (my + YS - y) % YS) * CORES + (mc + half) % CORES
            out_ref[g] = d[k * ROWS : (k + 1) * ROWS]

    decode(0, 0, 2 * far)
    for h in range(PIECES[1]):
        drain(part(1, 0, h), h_r.at[0, h])
    decode(1, 0, far)
    for h in range(PIECES[1]):
        drain(part(1, 1, h), h_r.at[1, h])
    decode(1, far, far)

    for wait in pending:
        wait()


def solution(mesh):
    def per_device(x, c, scale, e):
        t, width = x.shape
        rows = c.shape[0]
        cols = e.shape[1]
        n_grp = ZH * YS * CORES
        n_oct = len(OCTET) + 1
        n0, n1 = PIECES
        hbm = pl.BlockSpec(memory_space=pltpu.HBM)
        dma = pltpu.SemaphoreType.DMA
        x, c, e = (pltpu.with_memory_space_constraint(v, pltpu.HBM) for v in (x, c, e))
        return pl.pallas_call(
            kernel,
            out_shape=jax.ShapeDtypeStruct((n_grp, ROWS, cols), BF16),
            in_specs=[hbm, hbm, pl.BlockSpec(memory_space=pltpu.SMEM), hbm],
            out_specs=pl.BlockSpec(memory_space=pltpu.VMEM),
            scratch_shapes=[
                pltpu.VMEM((t, width), BF16),
                pltpu.VMEM((rows, width), F32),
                pltpu.VMEM((width, cols), BF16),
                pltpu.VMEM((2, ROWS, width), F32),
                pltpu.VMEM((2, ROWS, width), F32),
                pltpu.VMEM((2, n_grp - 1, 1, t), F32),
                pltpu.VMEM((2, 1, t), F32),
                pltpu.VMEM((2, n_oct, 1, rows), F32),
                pltpu.VMEM((2, 2, 1, rows), F32),
                pltpu.VMEM((2, 1, rows), F32),
                pltpu.VMEM((n0, 2, rows // 2, width // n0), BF16),
                pltpu.VMEM((n1, 2, rows // 2, width // n1), BF16),
                pltpu.VMEM((n0, n_oct, 2, ROWS, width // n0), BF16),
                pltpu.VMEM((n1, n_oct, 2, ROWS, width // n1), BF16),
                pltpu.VMEM((n0, 2, ROWS, width // n0), BF16),
                pltpu.VMEM((n0, 2, ROWS, width // n0), BF16),
                pltpu.VMEM((n1, ROWS, width // n1), BF16),
                pltpu.VMEM((n1, ROWS, width // n1), BF16),
                pltpu.VMEM((n0, 2, ROWS, width // n0), BF16),
                pltpu.VMEM((n0, 2, rows // 2, width // n0), BF16),
                pltpu.VMEM((1, rows), F32),
                pltpu.VMEM((n_oct, 1, rows), F32),
                pltpu.VMEM((2, n_grp // 2, ROWS, width), BF16),
                dma, dma, dma, dma, dma,
                dma((2,)), dma((2,)), dma((2,)), dma((2,)), dma((2,)), dma((2,)),
                dma((2, max(PIECES))), dma((2, max(PIECES))), dma((n0,)), dma((n0,)), dma((n1,)), dma((n1,)),
                dma((n0,)), dma((n0,)), dma, dma,
                dma((2, n1)), dma((2, n1)), dma, dma, dma((2, n1)), dma((2, n1)),
            ],
            compiler_params=pltpu.CompilerParams(
                collective_id=0, has_side_effects=True, vmem_limit_bytes=24 * 2**20
            ),
            name="kmeans_decode",
        )(x, c, scale, e)

    placed = (P("seq", None), P("grp", None), P(), P(None, "grp"))
    return jax.shard_map(
        per_device, mesh=mesh, in_specs=placed, out_specs=P(None, "seq", "grp"), check_vma=False
    )
```

```python
import functools

import jax
import jax.numpy as jnp
from jax import lax
from jax.experimental import pallas as pl
from jax.experimental.pallas import tpu as pltpu
from jax.sharding import PartitionSpec as P

MESH = pl.DeviceIdType.MESH
XS, ZL = 4, 4
ZH, YS, CORES = 2, 8, 2
ROWS = 16
F32, BF16 = jnp.float32, jnp.bfloat16
PIECES = (2, 2)


def ring(d, n):
    return min(d, n - d)


OCTET = sorted(
    [(z, x) for z in range(2) for x in range(XS) if z or x], key=lambda p: -(p[0] + ring(p[1], XS))
)
NEAR = sorted([(0, y) for y in range(1, YS)], key=lambda p: -ring(p[1], YS))
FAR = sorted([(1, y) for y in range(YS)], key=lambda p: -ring(p[1], YS))
CHIPS = FAR + NEAR


def seq_index(z, x):
    me = lax.axis_index("seq")
    mz, mx = me // XS, me % XS
    pz = ((mz // 2 + z // 2) % 2) * 2 + (mz % 2 + z % 2) % 2
    return pz * XS + (mx + x) % XS


def grp_index(z, y, c):
    me = lax.axis_index("grp")
    mc, my, mz = me % CORES, (me // CORES) % YS, me // (CORES * YS)
    return (((mz + z) % ZH) * YS + (my + y) % YS) * CORES + (mc + c) % CORES


def kernel(
    x_hbm, c_hbm, scale_ref, e_hbm, out_ref,
    x_ref, c_ref, e_ref, own, theirs_c, lse_near, lse_half, lse_buf, lse_src, mass_buf, mass_src, pair_mass,
    w_src0, w_src1, w_buf0, w_buf1, pair_src, pair_buf, last_src, last_buf, c_src, c_next, sq_src, sq_buf, fin,
    x_sem, c_sem, e_sem, a_s, a_r, b_s, b_r,
    lse_s, lse_r, m_s, m_r, n_s, n_r, w_s, w_r, o_s, o_r, l_s, l_r,
    c_s, c_r, q_s, q_r, f_s, f_r, p_s, p_r, h_s, h_r,
):
    tokens, width = x_hbm.shape
    rows = c_hbm.shape[0]
    w_src, w_buf = (w_src0, w_src1), (w_buf0, w_buf1)
    seq = lax.axis_index("seq")
    partner_group = grp_index(0, 0, 1)
    octet = [{"seq": seq_index(z, x), "grp": partner_group} for z, x in OCTET] + [{"grp": partner_group}]
    octet_index = [seq_index(z, x) % 8 for z, x in OCTET] + [seq % 8]
    across = {"seq": seq_index(2, 0)}
    peers_chip = [{"grp": grp_index(z, y, 0)} for z, y in CHIPS]
    peers_other = [{"grp": grp_index(z, y, 1)} for z, y in CHIPS]
    partner = {"grp": partner_group}
    near_both = [p for pair in zip(peers_chip[len(FAR) :], peers_other[len(FAR) :]) for p in pair] + [partner]
    opposite = {"grp": grp_index(1, 0, 1)}
    everyone = [opposite] + near_both + octet[:-1] + [across]

    barrier = pltpu.get_barrier_semaphore()
    for p in everyone:
        pl.semaphore_signal(barrier, inc=1, device_id=p, device_id_type=MESH)
    c_copy = pltpu.make_async_copy(c_hbm, c_ref, c_sem)
    c_copy.start()
    x_copy = pltpu.make_async_copy(x_hbm, x_ref, x_sem)
    x_copy.start()
    e_copy = pltpu.make_async_copy(e_hbm, e_ref, e_sem)
    e_copy.start()
    pending = [e_copy.wait]

    def send(src, dst, ssem, rsem, device):
        pltpu.make_async_remote_copy(
            src_ref=src, dst_ref=dst, send_sem=ssem, recv_sem=rsem,
            device_id=device, device_id_type=MESH,
        ).start()

    def drain(ref, sem):
        pltpu.make_async_copy(ref, ref, sem).wait()

    c_copy.wait()
    c0 = c_ref[...]
    half0 = 0.5 * jnp.sum(c0 * c0, axis=1, keepdims=True)
    factor = 2.0 / (scale_ref[0] * jnp.sqrt(jnp.float32(width)))
    x_copy.wait()
    size = [width // n for n in PIECES]
    cuts = [[slice(h * size[i], (h + 1) * size[i]) for h in range(n)] for i, n in enumerate(PIECES)]

    def merge(others, lse):
        m = jnp.maximum(jnp.max(others, axis=0), lse)
        return m + jnp.log(jnp.sum(jnp.exp(others - m[None]), axis=0) + jnp.exp(lse - m))

    def softmax(i, centres, half):
        dots = sum(
            lax.dot_general(
                centres[h], x_ref[:, cuts[0][h]], (((1,), (1,)), ((), ())), preferred_element_type=F32
            )
            for h in range(PIECES[0])
        )
        logits = factor * (dots - half)
        top = jnp.max(logits, axis=0, keepdims=True)
        lse = top + jnp.log(jnp.sum(jnp.exp(logits - top), axis=0, keepdims=True))
        lse_src[i] = lse
        if i == 0:
            pl.semaphore_wait(barrier, len(everyone))
        if i == 0:
            for slot, p in enumerate(near_both):
                send(lse_src.at[0], lse_near.at[slot], lse_s.at[0], lse_r.at[0], p)
            for q in range(2):
                start = pl.ds(pl.multiple_of(q * (rows // 2) + (seq % 8) * ROWS, ROWS), ROWS)
                send(c_ref.at[start], theirs_c.at[q], a_s, a_r, partner)
            pending.append(lambda: drain(lse_near, lse_s.at[0]))
            pending.append(lambda: drain(theirs_c, a_s))
            drain(lse_near, lse_r.at[0])
            near = merge(lse_near[...], lse)
            lse_half[0] = near
            send(lse_half.at[0], lse_half.at[1], b_s, b_r, opposite)
            pending.append(lambda: drain(lse_half.at[1], b_s))
            drain(lse_half.at[1], b_r)
            full = merge(lse_half[1:2], near)
        else:
            slot = 0
            for a, b in zip(peers_chip, peers_other):
                for p in (a, b):
                    send(lse_src.at[1], lse_buf.at[slot], lse_s.at[1], lse_r.at[1], p)
                    slot += 1
            send(lse_src.at[1], lse_buf.at[slot], lse_s.at[1], lse_r.at[1], partner)
            pending.append(lambda: drain(lse_buf, lse_s.at[1]))
            drain(lse_buf, lse_r.at[1])
            full = merge(lse_buf[...], lse)
        resp = jnp.exp(logits - full).astype(BF16)
        return resp

    n_oct = len(octet)
    j, hi = seq % 8, seq // 8
    lane = lax.broadcasted_iota(jnp.int32, (ROWS, rows), 1)
    row = lax.broadcasted_iota(jnp.int32, (ROWS, rows), 0)
    spots = [lane == q * (rows // 2) + j * ROWS + row for q in range(2)]

    def scatter(i, resp):
        for h, cut in enumerate(cuts[i]):
            w = jnp.dot(resp, x_ref[:, cut], preferred_element_type=F32)
            w_src[i][h] = w.astype(BF16).reshape(2, rows // 2, size[i])
            for k in range(n_oct):
                theirs = pl.ds(pl.multiple_of(octet_index[k] * ROWS, ROWS), ROWS)
                send(w_src[i].at[h, :, theirs], w_buf[i].at[h, k], w_s.at[i, h], w_r.at[i, h], octet[k])
            pending.append(lambda h=h: drain(w_buf[i].at[h], w_s.at[i, h]))
            if h == 0:
                mass = lax.dot_general(
                    jnp.ones((16, tokens), BF16), resp, (((1,), (1,)), ((), ())),
                    preferred_element_type=F32,
                )
                mass_src[i, 0] = mass[0:1]
                for k in range(n_oct):
                    send(mass_src.at[i, 0], mass_buf.at[i, k], m_s.at[i], m_r.at[i], octet[k])
                pending.append(lambda: drain(mass_buf.at[i], m_s.at[i]))

    def partial(i, h, side):
        acc = w_buf[i][h, 0, side].astype(F32)
        for k in range(1, n_oct):
            acc = acc + w_buf[i][h, k, side].astype(F32)
        return acc

    def pair_up_mass(i):
        drain(mass_buf.at[i], m_r.at[i])
        mass = jnp.sum(mass_buf[i], axis=0)
        mass_src[i, 1] = mass
        send(mass_src.at[i, 1], pair_mass.at[i], n_s.at[i], n_r.at[i], across)
        pending.append(lambda: drain(pair_mass.at[i], n_s.at[i]))
        return mass

    scatter(0, softmax(0, [c0[:, cut].astype(BF16) for cut in cuts[0]], half0))
    for h in range(PIECES[0]):
        drain(w_buf[0].at[h], w_r.at[0, h])
        for q in range(2):
            pair_src[h, q] = partial(0, h, q).astype(BF16)
        send(pair_src.at[h], pair_buf.at[h], o_s.at[h], o_r.at[h], across)
        pending.append(lambda h=h: drain(pair_buf.at[h], o_s.at[h]))
        if h == 0:
            mass = pair_up_mass(0)
    drain(pair_mass.at[0], n_r.at[0])
    mass = mass + pair_mass[0]
    bottoms = [jnp.sum(jnp.where(s, mass, 0.0), axis=1, keepdims=True) + 1.0 for s in spots]
    halves = [jnp.zeros((ROWS, 1), F32) for _ in range(2)]
    block = pl.ds(pl.multiple_of(j * ROWS, ROWS), ROWS)
    drain(theirs_c, a_r)
    for h, cut in enumerate(cuts[0]):
        drain(pair_buf.at[h], o_r.at[h])
        for q in range(2):
            both = pair_src[h, q].astype(F32) + pair_buf[h, q].astype(F32)
            centre = (both + theirs_c[q, :, cut]) / bottoms[q]
            own[q, :, cut] = centre
            c_src[h, q] = centre.astype(BF16)
            halves[q] += 0.5 * jnp.sum(centre * centre, axis=1, keepdims=True)
        for k in range(n_oct):
            send(c_src.at[h], c_next.at[h, :, block], c_s.at[h], c_r.at[h], octet[k])
        pending.append(lambda h=h: drain(c_next.at[h], c_s.at[h]))
    sq_src[...] = sum(
        jnp.sum(jnp.where(spots[q], halves[q], 0.0), axis=0, keepdims=True) for q in range(2)
    )
    for k in range(n_oct):
        send(sq_src, sq_buf.at[j], q_s, q_r, octet[k])
    pending.append(lambda: drain(sq_buf, q_s))
    for h in range(PIECES[0]):
        drain(c_next.at[h], c_r.at[h])
    drain(sq_buf, q_r)
    line = jnp.sum(sq_buf[...], axis=0)
    diagonal = lax.broadcasted_iota(jnp.int32, (rows, rows), 0) == lax.broadcasted_iota(
        jnp.int32, (rows, rows), 1
    )
    half1 = jnp.sum(jnp.where(diagonal, line, 0.0), axis=1, keepdims=True)

    scatter(1, softmax(1, [c_next[h].reshape(rows, size[0]) for h in range(PIECES[0])], half1))
    kept = []
    for h in range(PIECES[1]):
        drain(w_buf[1].at[h], w_r.at[1, h])
        last_src[h] = partial(1, h, 1 - hi).astype(BF16)
        send(last_src.at[h], last_buf.at[h], l_s.at[h], l_r.at[h], across)
        pending.append(lambda h=h: drain(last_buf.at[h], l_s.at[h]))
        kept.append(partial(1, h, hi))
        if h == 0:
            mass = pair_up_mass(1)
    drain(pair_mass.at[1], n_r.at[1])
    mass = mass + pair_mass[1]
    bottom = jnp.sum(jnp.where(lane == seq * ROWS + row, mass, 0.0), axis=1, keepdims=True) + 1.0

    def summed(h):
        drain(last_buf.at[h], l_r.at[h])
        return kept[h] + last_buf[h].astype(F32)

    near, far = len(NEAR), len(FAR)
    slots = [1 + near + k for k in range(far)] + [1 + k for k in range(near)]
    first, count = (1, 1 + near), (near, far)
    for h, cut in enumerate(cuts[1]):
        fin[1, 0, :, cut] = ((summed(h) + own[hi, :, cut]) / bottom).astype(BF16)
        lanes = pl.ds(cut.start, size[1])
        for k, slot in enumerate(slots):
            g = 1 if k < far else 0
            send(fin.at[1, 0, :, lanes], fin.at[0, slot, :, lanes], f_s.at[g, h], f_r.at[g, h], peers_other[k])
    send(fin.at[1, 0], fin.at[0, 0], p_s, p_r, partner)
    pending.append(lambda: drain(fin.at[0, 0], p_s))

    def part(c, g, h):
        return fin.at[c, pl.ds(first[g], count[g]), :, pl.ds(cuts[1][h].start, size[1])]

    for g in range(2):
        for h in range(PIECES[1]):
            pending.append(lambda g=g, h=h: drain(part(0, g, h), f_s.at[g, h]))
            drain(part(0, g, h), f_r.at[g, h])
            send(part(0, g, h), part(1, g, h), h_s.at[g, h], h_r.at[g, h], partner)
            pending.append(lambda g=g, h=h: drain(part(1, g, h), h_s.at[g, h]))
    pending.pop(0)()
    drain(fin.at[0, 0], p_r)
    me = lax.axis_index("grp")
    mc, my, mz = me % CORES, (me // CORES) % YS, me // (CORES * YS)
    chips = [(0, 0)] + NEAR + FAR

    def decode(half, first, count):
        part = fin[half, first : first + count].reshape(count * ROWS, width)
        d = jnp.dot(part, e_ref[...], preferred_element_type=F32).astype(BF16)
        for k in range(count):
            z, y = chips[first + k]
            g = (((mz + ZH - z) % ZH) * YS + (my + YS - y) % YS) * CORES + (mc + half) % CORES
            out_ref[g] = d[k * ROWS : (k + 1) * ROWS]

    decode(0, 0, 2 * far)
    for h in range(PIECES[1]):
        drain(part(1, 0, h), h_r.at[0, h])
    decode(1, 0, far)
    for h in range(PIECES[1]):
        drain(part(1, 1, h), h_r.at[1, h])
    decode(1, far, far)

    for wait in pending:
        wait()


def solution(mesh):
    def per_device(x, c, scale, e):
        t, width = x.shape
        rows = c.shape[0]
        cols = e.shape[1]
        n_grp = ZH * YS * CORES
        n_oct = len(OCTET) + 1
        n0, n1 = PIECES
        hbm = pl.BlockSpec(memory_space=pltpu.HBM)
        dma = pltpu.SemaphoreType.DMA
        x, c, e = (pltpu.with_memory_space_constraint(v, pltpu.HBM) for v in (x, c, e))
        return pl.pallas_call(
            kernel,
            out_shape=jax.ShapeDtypeStruct((n_grp, ROWS, cols), BF16),
            in_specs=[hbm, hbm, pl.BlockSpec(memory_space=pltpu.SMEM), hbm],
            out_specs=pl.BlockSpec(memory_space=pltpu.VMEM),
            scratch_shapes=[
                pltpu.VMEM((t, width), BF16),
                pltpu.VMEM((rows, width), F32),
                pltpu.VMEM((width, cols), BF16),
                pltpu.VMEM((2, ROWS, width), F32),
                pltpu.VMEM((2, ROWS, width), F32),
                pltpu.VMEM((n_grp // 2 - 1, 1, t), F32),
                pltpu.VMEM((2, 1, t), F32),
                pltpu.VMEM((n_grp - 1, 1, t), F32),
                pltpu.VMEM((2, 1, t), F32),
                pltpu.VMEM((2, n_oct, 1, rows), F32),
                pltpu.VMEM((2, 2, 1, rows), F32),
                pltpu.VMEM((2, 1, rows), F32),
                pltpu.VMEM((n0, 2, rows // 2, width // n0), BF16),
                pltpu.VMEM((n1, 2, rows // 2, width // n1), BF16),
                pltpu.VMEM((n0, n_oct, 2, ROWS, width // n0), BF16),
                pltpu.VMEM((n1, n_oct, 2, ROWS, width // n1), BF16),
                pltpu.VMEM((n0, 2, ROWS, width // n0), BF16),
                pltpu.VMEM((n0, 2, ROWS, width // n0), BF16),
                pltpu.VMEM((n1, ROWS, width // n1), BF16),
                pltpu.VMEM((n1, ROWS, width // n1), BF16),
                pltpu.VMEM((n0, 2, ROWS, width // n0), BF16),
                pltpu.VMEM((n0, 2, rows // 2, width // n0), BF16),
                pltpu.VMEM((1, rows), F32),
                pltpu.VMEM((n_oct, 1, rows), F32),
                pltpu.VMEM((2, n_grp // 2, ROWS, width), BF16),
                dma, dma, dma, dma, dma, dma, dma,
                dma((2,)), dma((2,)), dma((2,)), dma((2,)), dma((2,)), dma((2,)),
                dma((2, max(PIECES))), dma((2, max(PIECES))), dma((n0,)), dma((n0,)), dma((n1,)), dma((n1,)),
                dma((n0,)), dma((n0,)), dma, dma,
                dma((2, n1)), dma((2, n1)), dma, dma, dma((2, n1)), dma((2, n1)),
            ],
            compiler_params=pltpu.CompilerParams(
                collective_id=0, has_side_effects=True, vmem_limit_bytes=24 * 2**20
            ),
            name="kmeans_decode",
        )(x, c, scale, e)

    placed = (P("seq", None), P("grp", None), P(), P(None, "grp"))
    return jax.shard_map(
        per_device, mesh=mesh, in_specs=placed, out_specs=P(None, "seq", "grp"), check_vma=False
    )
```

```python
import functools

import jax
import jax.numpy as jnp
from jax import lax
from jax.experimental import pallas as pl
from jax.experimental.pallas import tpu as pltpu
from jax.sharding import PartitionSpec as P

MESH = pl.DeviceIdType.MESH
XS, ZL = 4, 4
ZH, YS, CORES = 2, 8, 2
ROWS = 16
F32, BF16 = jnp.float32, jnp.bfloat16
PIECES = (2, 2)


def ring(d, n):
    return min(d, n - d)


OCTET = sorted(
    [(z, x) for z in range(2) for x in range(XS) if z or x], key=lambda p: -(p[0] + ring(p[1], XS))
)
NEAR = sorted([(0, y) for y in range(1, YS)], key=lambda p: -ring(p[1], YS))
FAR = sorted([(1, y) for y in range(YS)], key=lambda p: -ring(p[1], YS))
CHIPS = FAR + NEAR


def seq_index(z, x):
    me = lax.axis_index("seq")
    mz, mx = me // XS, me % XS
    pz = ((mz // 2 + z // 2) % 2) * 2 + (mz % 2 + z % 2) % 2
    return pz * XS + (mx + x) % XS


def grp_index(z, y, c):
    me = lax.axis_index("grp")
    mc, my, mz = me % CORES, (me // CORES) % YS, me // (CORES * YS)
    return (((mz + z) % ZH) * YS + (my + y) % YS) * CORES + (mc + c) % CORES


def kernel(
    x_hbm, c_hbm, scale_ref, e_hbm, out_ref,
    x_ref, c_ref, e_ref, own, theirs_c, lse_buf, lse_src, mass_buf, mass_src, pair_mass,
    w_src0, w_src1, w_buf0, w_buf1, pair_src, pair_buf, last_src, last_buf, c_src, c_next, sq_src, sq_buf, fin,
    x_sem, c_sem, e_sem, a_s, a_r,
    lse_s, lse_r, m_s, m_r, n_s, n_r, w_s, w_r, o_s, o_r, l_s, l_r,
    c_s, c_r, q_s, q_r, f_s, f_r, p_s, p_r, h_s, h_r,
):
    tokens, width = x_hbm.shape
    rows = c_hbm.shape[0]
    w_src, w_buf = (w_src0, w_src1), (w_buf0, w_buf1)
    seq = lax.axis_index("seq")
    partner_group = grp_index(0, 0, 1)
    octet = [{"seq": seq_index(z, x), "grp": partner_group} for z, x in OCTET] + [{"grp": partner_group}]
    octet_index = [seq_index(z, x) % 8 for z, x in OCTET] + [seq % 8]
    across = {"seq": seq_index(2, 0)}
    peers_chip = [{"grp": grp_index(z, y, 0)} for z, y in CHIPS]
    peers_other = [{"grp": grp_index(z, y, 1)} for z, y in CHIPS]
    partner = {"grp": partner_group}
    everyone = [p for pair in zip(peers_chip, peers_other) for p in pair] + octet + [across]

    barrier = pltpu.get_barrier_semaphore()
    for p in everyone:
        pl.semaphore_signal(barrier, inc=1, device_id=p, device_id_type=MESH)
    c_copy = pltpu.make_async_copy(c_hbm, c_ref, c_sem)
    c_copy.start()
    x_copy = pltpu.make_async_copy(x_hbm, x_ref, x_sem)
    x_copy.start()
    e_copy = pltpu.make_async_copy(e_hbm, e_ref, e_sem)
    e_copy.start()
    pending = [e_copy.wait]

    def send(src, dst, ssem, rsem, device):
        pltpu.make_async_remote_copy(
            src_ref=src, dst_ref=dst, send_sem=ssem, recv_sem=rsem,
            device_id=device, device_id_type=MESH,
        ).start()

    def drain(ref, sem):
        pltpu.make_async_copy(ref, ref, sem).wait()

    c_copy.wait()
    c0 = c_ref[...]
    half0 = 0.5 * jnp.sum(c0 * c0, axis=1, keepdims=True)
    factor = 2.0 / (scale_ref[0] * jnp.sqrt(jnp.float32(width)))
    x_copy.wait()
    size = [width // n for n in PIECES]
    cuts = [[slice(h * size[i], (h + 1) * size[i]) for h in range(n)] for i, n in enumerate(PIECES)]

    def softmax(i, centres, half):
        dots = sum(
            lax.dot_general(
                centres[h], x_ref[:, cuts[0][h]], (((1,), (1,)), ((), ())), preferred_element_type=F32
            )
            for h in range(PIECES[0])
        )
        logits = factor * (dots - half)
        top = jnp.max(logits, axis=0, keepdims=True)
        weights = jnp.exp(logits - top)
        lse = top + jnp.log(jnp.sum(weights, axis=0, keepdims=True))
        lse_src[i] = lse
        if i == 0:
            pl.semaphore_wait(barrier, len(everyone))
        slot = 0
        for a, b in zip(peers_chip, peers_other):
            for p in (a, b):
                send(lse_src.at[i], lse_buf.at[i, slot], lse_s.at[i], lse_r.at[i], p)
                slot += 1
        send(lse_src.at[i], lse_buf.at[i, slot], lse_s.at[i], lse_r.at[i], partner)
        pending.append(lambda: drain(lse_buf.at[i], lse_s.at[i]))
        if i == 0:
            for q in range(2):
                start = pl.ds(pl.multiple_of(q * (rows // 2) + (seq % 8) * ROWS, ROWS), ROWS)
                send(c_ref.at[start], theirs_c.at[q], a_s, a_r, partner)
            pending.append(lambda: drain(theirs_c, a_s))
        drain(lse_buf.at[i], lse_r.at[i])
        others = lse_buf[i]
        m = jnp.maximum(jnp.max(others, axis=0), lse)
        total = jnp.sum(jnp.exp(others - m[None]), axis=0) + jnp.exp(lse - m)
        full = m + jnp.log(total)
        resp = (weights * jnp.exp(top - full)).astype(BF16)
        return resp

    n_oct = len(octet)
    j, hi = seq % 8, seq // 8
    lane = lax.broadcasted_iota(jnp.int32, (ROWS, rows), 1)
    row = lax.broadcasted_iota(jnp.int32, (ROWS, rows), 0)
    spots = [lane == q * (rows // 2) + j * ROWS + row for q in range(2)]

    def scatter(i, resp):
        for h, cut in enumerate(cuts[i]):
            w = jnp.dot(resp, x_ref[:, cut], preferred_element_type=F32)
            w_src[i][h] = w.astype(BF16).reshape(2, rows // 2, size[i])
            for k in range(n_oct):
                theirs = pl.ds(pl.multiple_of(octet_index[k] * ROWS, ROWS), ROWS)
                send(w_src[i].at[h, :, theirs], w_buf[i].at[h, k], w_s.at[i, h], w_r.at[i, h], octet[k])
            pending.append(lambda h=h: drain(w_buf[i].at[h], w_s.at[i, h]))
            if h == 0:
                mass = lax.dot_general(
                    jnp.ones((16, tokens), BF16), resp, (((1,), (1,)), ((), ())),
                    preferred_element_type=F32,
                )
                mass_src[i, 0] = mass[0:1]
                for k in range(n_oct):
                    send(mass_src.at[i, 0], mass_buf.at[i, k], m_s.at[i], m_r.at[i], octet[k])
                pending.append(lambda: drain(mass_buf.at[i], m_s.at[i]))

    def partial(i, h, side):
        acc = w_buf[i][h, 0, side].astype(F32)
        for k in range(1, n_oct):
            acc = acc + w_buf[i][h, k, side].astype(F32)
        return acc

    def pair_up_mass(i):
        drain(mass_buf.at[i], m_r.at[i])
        mass = jnp.sum(mass_buf[i], axis=0)
        mass_src[i, 1] = mass
        send(mass_src.at[i, 1], pair_mass.at[i], n_s.at[i], n_r.at[i], across)
        pending.append(lambda: drain(pair_mass.at[i], n_s.at[i]))
        return mass

    scatter(0, softmax(0, [c0[:, cut].astype(BF16) for cut in cuts[0]], half0))
    for h in range(PIECES[0]):
        drain(w_buf[0].at[h], w_r.at[0, h])
        for q in range(2):
            pair_src[h, q] = partial(0, h, q).astype(BF16)
        send(pair_src.at[h], pair_buf.at[h], o_s.at[h], o_r.at[h], across)
        pending.append(lambda h=h: drain(pair_buf.at[h], o_s.at[h]))
        if h == 0:
            mass = pair_up_mass(0)
    drain(pair_mass.at[0], n_r.at[0])
    mass = mass + pair_mass[0]
    bottoms = [jnp.sum(jnp.where(s, mass, 0.0), axis=1, keepdims=True) + 1.0 for s in spots]
    halves = [jnp.zeros((ROWS, 1), F32) for _ in range(2)]
    block = pl.ds(pl.multiple_of(j * ROWS, ROWS), ROWS)
    drain(theirs_c, a_r)
    for h, cut in enumerate(cuts[0]):
        drain(pair_buf.at[h], o_r.at[h])
        for q in range(2):
            both = pair_src[h, q].astype(F32) + pair_buf[h, q].astype(F32)
            centre = (both + theirs_c[q, :, cut]) / bottoms[q]
            own[q, :, cut] = centre
            c_src[h, q] = centre.astype(BF16)
            halves[q] += 0.5 * jnp.sum(centre * centre, axis=1, keepdims=True)
        for k in range(n_oct):
            send(c_src.at[h], c_next.at[h, :, block], c_s.at[h], c_r.at[h], octet[k])
        pending.append(lambda h=h: drain(c_next.at[h], c_s.at[h]))
    sq_src[...] = sum(
        jnp.sum(jnp.where(spots[q], halves[q], 0.0), axis=0, keepdims=True) for q in range(2)
    )
    for k in range(n_oct):
        send(sq_src, sq_buf.at[j], q_s, q_r, octet[k])
    pending.append(lambda: drain(sq_buf, q_s))
    for h in range(PIECES[0]):
        drain(c_next.at[h], c_r.at[h])
    drain(sq_buf, q_r)
    line = jnp.sum(sq_buf[...], axis=0)
    diagonal = lax.broadcasted_iota(jnp.int32, (rows, rows), 0) == lax.broadcasted_iota(
        jnp.int32, (rows, rows), 1
    )
    half1 = jnp.sum(jnp.where(diagonal, line, 0.0), axis=1, keepdims=True)

    scatter(1, softmax(1, [c_next[h].reshape(rows, size[0]) for h in range(PIECES[0])], half1))
    kept = []
    for h in range(PIECES[1]):
        drain(w_buf[1].at[h], w_r.at[1, h])
        last_src[h] = partial(1, h, 1 - hi).astype(BF16)
        send(last_src.at[h], last_buf.at[h], l_s.at[h], l_r.at[h], across)
        pending.append(lambda h=h: drain(last_buf.at[h], l_s.at[h]))
        kept.append(partial(1, h, hi))
        if h == 0:
            mass = pair_up_mass(1)
    drain(pair_mass.at[1], n_r.at[1])
    mass = mass + pair_mass[1]
    bottom = jnp.sum(jnp.where(lane == seq * ROWS + row, mass, 0.0), axis=1, keepdims=True) + 1.0

    def summed(h):
        drain(last_buf.at[h], l_r.at[h])
        return kept[h] + last_buf[h].astype(F32)

    near, far = len(NEAR), len(FAR)
    slots = [1 + near + k for k in range(far)] + [1 + k for k in range(near)]
    first, count = (1, 1 + near), (near, far)
    for h, cut in enumerate(cuts[1]):
        fin[1, 0, :, cut] = ((summed(h) + own[hi, :, cut]) / bottom).astype(BF16)
        lanes = pl.ds(cut.start, size[1])
        for k, slot in enumerate(slots):
            g = 1 if k < far else 0
            send(fin.at[1, 0, :, lanes], fin.at[0, slot, :, lanes], f_s.at[g, h], f_r.at[g, h], peers_other[k])
    send(fin.at[1, 0], fin.at[0, 0], p_s, p_r, partner)
    pending.append(lambda: drain(fin.at[0, 0], p_s))

    def part(c, g, h):
        return fin.at[c, pl.ds(first[g], count[g]), :, pl.ds(cuts[1][h].start, size[1])]

    for g in range(2):
        for h in range(PIECES[1]):
            pending.append(lambda g=g, h=h: drain(part(0, g, h), f_s.at[g, h]))
            drain(part(0, g, h), f_r.at[g, h])
            send(part(0, g, h), part(1, g, h), h_s.at[g, h], h_r.at[g, h], partner)
            pending.append(lambda g=g, h=h: drain(part(1, g, h), h_s.at[g, h]))
    pending.pop(0)()
    drain(fin.at[0, 0], p_r)
    me = lax.axis_index("grp")
    mc, my, mz = me % CORES, (me // CORES) % YS, me // (CORES * YS)
    chips = [(0, 0)] + NEAR + FAR

    def place(half, first, count, d):
        for k in range(count):
            z, y = chips[first + k]
            g = (((mz + ZH - z) % ZH) * YS + (my + YS - y) % YS) * CORES + (mc + half) % CORES
            out_ref[g] = d[k * ROWS : (k + 1) * ROWS]

    def decode(half, first, count):
        part = fin[half, first : first + count].reshape(count * ROWS, width)
        d = jnp.dot(part, e_ref[...], preferred_element_type=F32).astype(BF16)
        place(half, first, count, d)

    decode(0, 0, 2 * far)
    for h in range(PIECES[1]):
        drain(part(1, 0, h), h_r.at[0, h])
    decode(1, 0, far)
    d = None
    for h, cut in enumerate(cuts[1]):
        drain(part(1, 1, h), h_r.at[1, h])
        rows_h = fin[1, far : 2 * far, :, cut].reshape(far * ROWS, size[1])
        d_h = jnp.dot(rows_h, e_ref[cut, :], preferred_element_type=F32)
        d = d_h if d is None else d + d_h
    place(1, far, far, d.astype(BF16))

    for wait in pending:
        wait()


def solution(mesh):
    def per_device(x, c, scale, e):
        t, width = x.shape
        rows = c.shape[0]
        cols = e.shape[1]
        n_grp = ZH * YS * CORES
        n_oct = len(OCTET) + 1
        n0, n1 = PIECES
        hbm = pl.BlockSpec(memory_space=pltpu.HBM)
        dma = pltpu.SemaphoreType.DMA
        x, c, e = (pltpu.with_memory_space_constraint(v, pltpu.HBM) for v in (x, c, e))
        return pl.pallas_call(
            kernel,
            out_shape=jax.ShapeDtypeStruct((n_grp, ROWS, cols), BF16),
            in_specs=[hbm, hbm, pl.BlockSpec(memory_space=pltpu.SMEM), hbm],
            out_specs=pl.BlockSpec(memory_space=pltpu.VMEM),
            scratch_shapes=[
                pltpu.VMEM((t, width), BF16),
                pltpu.VMEM((rows, width), F32),
                pltpu.VMEM((width, cols), BF16),
                pltpu.VMEM((2, ROWS, width), F32),
                pltpu.VMEM((2, ROWS, width), F32),
                pltpu.VMEM((2, n_grp - 1, 1, t), F32),
                pltpu.VMEM((2, 1, t), F32),
                pltpu.VMEM((2, n_oct, 1, rows), F32),
                pltpu.VMEM((2, 2, 1, rows), F32),
                pltpu.VMEM((2, 1, rows), F32),
                pltpu.VMEM((n0, 2, rows // 2, width // n0), BF16),
                pltpu.VMEM((n1, 2, rows // 2, width // n1), BF16),
                pltpu.VMEM((n0, n_oct, 2, ROWS, width // n0), BF16),
                pltpu.VMEM((n1, n_oct, 2, ROWS, width // n1), BF16),
                pltpu.VMEM((n0, 2, ROWS, width // n0), BF16),
                pltpu.VMEM((n0, 2, ROWS, width // n0), BF16),
                pltpu.VMEM((n1, ROWS, width // n1), BF16),
                pltpu.VMEM((n1, ROWS, width // n1), BF16),
                pltpu.VMEM((n0, 2, ROWS, width // n0), BF16),
                pltpu.VMEM((n0, 2, rows // 2, width // n0), BF16),
                pltpu.VMEM((1, rows), F32),
                pltpu.VMEM((n_oct, 1, rows), F32),
                pltpu.VMEM((2, n_grp // 2, ROWS, width), BF16),
                dma, dma, dma, dma, dma,
                dma((2,)), dma((2,)), dma((2,)), dma((2,)), dma((2,)), dma((2,)),
                dma((2, max(PIECES))), dma((2, max(PIECES))), dma((n0,)), dma((n0,)), dma((n1,)), dma((n1,)),
                dma((n0,)), dma((n0,)), dma, dma,
                dma((2, n1)), dma((2, n1)), dma, dma, dma((2, n1)), dma((2, n1)),
            ],
            compiler_params=pltpu.CompilerParams(
                collective_id=0, has_side_effects=True, vmem_limit_bytes=24 * 2**20
            ),
            name="kmeans_decode",
        )(x, c, scale, e)

    placed = (P("seq", None), P("grp", None), P(), P(None, "grp"))
    return jax.shard_map(
        per_device, mesh=mesh, in_specs=placed, out_specs=P(None, "seq", "grp"), check_vma=False
    )
```

```python
import functools

import jax
import jax.numpy as jnp
from jax import lax
from jax.experimental import pallas as pl
from jax.experimental.pallas import tpu as pltpu
from jax.sharding import PartitionSpec as P

MESH = pl.DeviceIdType.MESH
XS, ZL = 4, 4
ZH, YS, CORES = 2, 8, 2
ROWS = 16
F32, BF16 = jnp.float32, jnp.bfloat16
PIECES = (4, 2)


def ring(d, n):
    return min(d, n - d)


OCTET = sorted(
    [(z, x) for z in range(2) for x in range(XS) if z or x], key=lambda p: -(p[0] + ring(p[1], XS))
)
NEAR = sorted([(0, y) for y in range(1, YS)], key=lambda p: -ring(p[1], YS))
FAR = sorted([(1, y) for y in range(YS)], key=lambda p: -ring(p[1], YS))
CHIPS = FAR + NEAR


def seq_index(z, x):
    me = lax.axis_index("seq")
    mz, mx = me // XS, me % XS
    pz = ((mz // 2 + z // 2) % 2) * 2 + (mz % 2 + z % 2) % 2
    return pz * XS + (mx + x) % XS


def grp_index(z, y, c):
    me = lax.axis_index("grp")
    mc, my, mz = me % CORES, (me // CORES) % YS, me // (CORES * YS)
    return (((mz + z) % ZH) * YS + (my + y) % YS) * CORES + (mc + c) % CORES


def kernel(
    x_hbm, c_hbm, scale_ref, e_hbm, out_ref,
    x_ref, c_ref, e_ref, own, theirs_c, lse_buf, lse_src, mass_buf, mass_src, pair_mass,
    w_src0, w_src1, w_buf0, w_buf1, pair_src, pair_buf, last_src, last_buf, c_src, c_next, sq_src, sq_buf, fin,
    x_sem, c_sem, e_sem, a_s, a_r,
    lse_s, lse_r, m_s, m_r, n_s, n_r, w_s, w_r, o_s, o_r, l_s, l_r,
    c_s, c_r, q_s, q_r, f_s, f_r, p_s, p_r, h_s, h_r,
):
    tokens, width = x_hbm.shape
    rows = c_hbm.shape[0]
    w_src, w_buf = (w_src0, w_src1), (w_buf0, w_buf1)
    seq = lax.axis_index("seq")
    partner_group = grp_index(0, 0, 1)
    octet = [{"seq": seq_index(z, x), "grp": partner_group} for z, x in OCTET] + [{"grp": partner_group}]
    octet_index = [seq_index(z, x) % 8 for z, x in OCTET] + [seq % 8]
    across = {"seq": seq_index(2, 0)}
    peers_chip = [{"grp": grp_index(z, y, 0)} for z, y in CHIPS]
    peers_other = [{"grp": grp_index(z, y, 1)} for z, y in CHIPS]
    partner = {"grp": partner_group}
    everyone = [p for pair in zip(peers_chip, peers_other) for p in pair] + octet + [across]

    c_copy = pltpu.make_async_copy(c_hbm, c_ref, c_sem)
    c_copy.start()
    x_copy = pltpu.make_async_copy(x_hbm, x_ref, x_sem)
    x_copy.start()
    barrier = pltpu.get_barrier_semaphore()
    for p in everyone:
        pl.semaphore_signal(barrier, inc=1, device_id=p, device_id_type=MESH)
    e_copy = pltpu.make_async_copy(e_hbm, e_ref, e_sem)
    e_copy.start()
    pending = [e_copy.wait]

    def send(src, dst, ssem, rsem, device):
        pltpu.make_async_remote_copy(
            src_ref=src, dst_ref=dst, send_sem=ssem, recv_sem=rsem,
            device_id=device, device_id_type=MESH,
        ).start()

    def drain(ref, sem):
        pltpu.make_async_copy(ref, ref, sem).wait()

    c_copy.wait()
    c0 = c_ref[...]
    half0 = 0.5 * jnp.sum(c0 * c0, axis=1, keepdims=True)
    factor = 2.0 / (scale_ref[0] * jnp.sqrt(jnp.float32(width)))
    x_copy.wait()
    size = [width // n for n in PIECES]
    cuts = [[slice(h * size[i], (h + 1) * size[i]) for h in range(n)] for i, n in enumerate(PIECES)]

    def softmax(i, centres, half):
        dots = sum(
            lax.dot_general(
                centres[h], x_ref[:, cuts[0][h]], (((1,), (1,)), ((), ())), preferred_element_type=F32
            )
            for h in range(PIECES[0])
        )
        logits = factor * (dots - half)
        top = jnp.max(logits, axis=0, keepdims=True)
        lse = top + jnp.log(jnp.sum(jnp.exp(logits - top), axis=0, keepdims=True))
        lse_src[i] = lse
        if i == 0:
            pl.semaphore_wait(barrier, len(everyone))
        slot = 0
        for a, b in zip(peers_chip, peers_other):
            for p in (a, b):
                send(lse_src.at[i], lse_buf.at[i, slot], lse_s.at[i], lse_r.at[i], p)
                slot += 1
        send(lse_src.at[i], lse_buf.at[i, slot], lse_s.at[i], lse_r.at[i], partner)
        pending.append(lambda: drain(lse_buf.at[i], lse_s.at[i]))
        if i == 0:
            for q in range(2):
                start = pl.ds(pl.multiple_of(q * (rows // 2) + (seq % 8) * ROWS, ROWS), ROWS)
                send(c_ref.at[start], theirs_c.at[q], a_s, a_r, partner)
            pending.append(lambda: drain(theirs_c, a_s))
        drain(lse_buf.at[i], lse_r.at[i])
        others = lse_buf[i]
        m = jnp.maximum(jnp.max(others, axis=0), lse)
        total = jnp.sum(jnp.exp(others - m[None]), axis=0) + jnp.exp(lse - m)
        full = m + jnp.log(total)
        resp = jnp.exp(logits - full).astype(BF16)
        return resp

    n_oct = len(octet)
    j, hi = seq % 8, seq // 8
    lane = lax.broadcasted_iota(jnp.int32, (ROWS, rows), 1)
    row = lax.broadcasted_iota(jnp.int32, (ROWS, rows), 0)
    spots = [lane == q * (rows // 2) + j * ROWS + row for q in range(2)]

    def scatter(i, resp):
        for h, cut in enumerate(cuts[i]):
            w = jnp.dot(resp, x_ref[:, cut], preferred_element_type=F32)
            w_src[i][h] = w.astype(BF16).reshape(2, rows // 2, size[i])
            for k in range(n_oct):
                theirs = pl.ds(pl.multiple_of(octet_index[k] * ROWS, ROWS), ROWS)
                send(w_src[i].at[h, :, theirs], w_buf[i].at[h, k], w_s.at[i, h], w_r.at[i, h], octet[k])
            pending.append(lambda h=h: drain(w_buf[i].at[h], w_s.at[i, h]))
            if h == 0:
                mass = lax.dot_general(
                    jnp.ones((16, tokens), BF16), resp, (((1,), (1,)), ((), ())),
                    preferred_element_type=F32,
                )
                mass_src[i, 0] = mass[0:1]
                for k in range(n_oct):
                    send(mass_src.at[i, 0], mass_buf.at[i, k], m_s.at[i], m_r.at[i], octet[k])
                pending.append(lambda: drain(mass_buf.at[i], m_s.at[i]))

    def partial(i, h, side):
        acc = w_buf[i][h, 0, side].astype(F32)
        for k in range(1, n_oct):
            acc = acc + w_buf[i][h, k, side].astype(F32)
        return acc

    def pair_up_mass(i):
        drain(mass_buf.at[i], m_r.at[i])
        mass = jnp.sum(mass_buf[i], axis=0)
        mass_src[i, 1] = mass
        send(mass_src.at[i, 1], pair_mass.at[i], n_s.at[i], n_r.at[i], across)
        pending.append(lambda: drain(pair_mass.at[i], n_s.at[i]))
        return mass

    scatter(0, softmax(0, [c0[:, cut].astype(BF16) for cut in cuts[0]], half0))
    for h in range(PIECES[0]):
        drain(w_buf[0].at[h], w_r.at[0, h])
        for q in range(2):
            pair_src[h, q] = partial(0, h, q).astype(BF16)
        send(pair_src.at[h], pair_buf.at[h], o_s.at[h], o_r.at[h], across)
        pending.append(lambda h=h: drain(pair_buf.at[h], o_s.at[h]))
        if h == 0:
            mass = pair_up_mass(0)
    drain(pair_mass.at[0], n_r.at[0])
    mass = mass + pair_mass[0]
    bottoms = [jnp.sum(jnp.where(s, mass, 0.0), axis=1, keepdims=True) + 1.0 for s in spots]
    halves = [jnp.zeros((ROWS, 1), F32) for _ in range(2)]
    block = pl.ds(pl.multiple_of(j * ROWS, ROWS), ROWS)
    drain(theirs_c, a_r)
    for h, cut in enumerate(cuts[0]):
        drain(pair_buf.at[h], o_r.at[h])
        for q in range(2):
            both = pair_src[h, q].astype(F32) + pair_buf[h, q].astype(F32)
            centre = (both + theirs_c[q, :, cut]) / bottoms[q]
            own[q, :, cut] = centre
            c_src[h, q] = centre.astype(BF16)
            halves[q] += 0.5 * jnp.sum(centre * centre, axis=1, keepdims=True)
        for k in range(n_oct):
            send(c_src.at[h], c_next.at[h, :, block], c_s.at[h], c_r.at[h], octet[k])
        pending.append(lambda h=h: drain(c_next.at[h], c_s.at[h]))
    sq_src[...] = sum(
        jnp.sum(jnp.where(spots[q], halves[q], 0.0), axis=0, keepdims=True) for q in range(2)
    )
    for k in range(n_oct):
        send(sq_src, sq_buf.at[j], q_s, q_r, octet[k])
    pending.append(lambda: drain(sq_buf, q_s))
    for h in range(PIECES[0]):
        drain(c_next.at[h], c_r.at[h])
    drain(sq_buf, q_r)
    line = jnp.sum(sq_buf[...], axis=0)
    diagonal = lax.broadcasted_iota(jnp.int32, (rows, rows), 0) == lax.broadcasted_iota(
        jnp.int32, (rows, rows), 1
    )
    half1 = jnp.sum(jnp.where(diagonal, line, 0.0), axis=1, keepdims=True)

    scatter(1, softmax(1, [c_next[h].reshape(rows, size[0]) for h in range(PIECES[0])], half1))
    kept = []
    for h in range(PIECES[1]):
        drain(w_buf[1].at[h], w_r.at[1, h])
        last_src[h] = partial(1, h, 1 - hi).astype(BF16)
        send(last_src.at[h], last_buf.at[h], l_s.at[h], l_r.at[h], across)
        pending.append(lambda h=h: drain(last_buf.at[h], l_s.at[h]))
        kept.append(partial(1, h, hi))
        if h == 0:
            mass = pair_up_mass(1)
    drain(pair_mass.at[1], n_r.at[1])
    mass = mass + pair_mass[1]
    bottom = jnp.sum(jnp.where(lane == seq * ROWS + row, mass, 0.0), axis=1, keepdims=True) + 1.0

    def summed(h):
        drain(last_buf.at[h], l_r.at[h])
        return kept[h] + last_buf[h].astype(F32)

    near, far = len(NEAR), len(FAR)
    slots = [1 + near + k for k in range(far)] + [1 + k for k in range(near)]
    first, count = (1, 1 + near), (near, far)
    for h, cut in enumerate(cuts[1]):
        fin[1, 0, :, cut] = ((summed(h) + own[hi, :, cut]) / bottom).astype(BF16)
        lanes = pl.ds(cut.start, size[1])
        for k, slot in enumerate(slots):
            g = 1 if k < far else 0
            send(fin.at[1, 0, :, lanes], fin.at[0, slot, :, lanes], f_s.at[g, h], f_r.at[g, h], peers_other[k])
    send(fin.at[1, 0], fin.at[0, 0], p_s, p_r, partner)
    pending.append(lambda: drain(fin.at[0, 0], p_s))

    def part(c, g, h):
        return fin.at[c, pl.ds(first[g], count[g]), :, pl.ds(cuts[1][h].start, size[1])]

    for g in range(2):
        for h in range(PIECES[1]):
            pending.append(lambda g=g, h=h: drain(part(0, g, h), f_s.at[g, h]))
            drain(part(0, g, h), f_r.at[g, h])
            send(part(0, g, h), part(1, g, h), h_s.at[g, h], h_r.at[g, h], partner)
            pending.append(lambda g=g, h=h: drain(part(1, g, h), h_s.at[g, h]))
    pending.pop(0)()
    drain(fin.at[0, 0], p_r)
    me = lax.axis_index("grp")
    mc, my, mz = me % CORES, (me // CORES) % YS, me // (CORES * YS)
    chips = [(0, 0)] + NEAR + FAR

    def decode(half, first, count):
        part = fin[half, first : first + count].reshape(count * ROWS, width)
        d = jnp.dot(part, e_ref[...], preferred_element_type=F32).astype(BF16)
        for k in range(count):
            z, y = chips[first + k]
            g = (((mz + ZH - z) % ZH) * YS + (my + YS - y) % YS) * CORES + (mc + half) % CORES
            out_ref[g] = d[k * ROWS : (k + 1) * ROWS]

    decode(0, 0, 2 * far)
    for h in range(PIECES[1]):
        drain(part(1, 0, h), h_r.at[0, h])
    decode(1, 0, far)
    for h in range(PIECES[1]):
        drain(part(1, 1, h), h_r.at[1, h])
    decode(1, far, far)

    for wait in pending:
        wait()


def solution(mesh):
    def per_device(x, c, scale, e):
        t, width = x.shape
        rows = c.shape[0]
        cols = e.shape[1]
        n_grp = ZH * YS * CORES
        n_oct = len(OCTET) + 1
        n0, n1 = PIECES
        hbm = pl.BlockSpec(memory_space=pltpu.HBM)
        dma = pltpu.SemaphoreType.DMA
        x, c, e = (pltpu.with_memory_space_constraint(v, pltpu.HBM) for v in (x, c, e))
        return pl.pallas_call(
            kernel,
            out_shape=jax.ShapeDtypeStruct((n_grp, ROWS, cols), BF16),
            in_specs=[hbm, hbm, pl.BlockSpec(memory_space=pltpu.SMEM), hbm],
            out_specs=pl.BlockSpec(memory_space=pltpu.VMEM),
            scratch_shapes=[
                pltpu.VMEM((t, width), BF16),
                pltpu.VMEM((rows, width), F32),
                pltpu.VMEM((width, cols), BF16),
                pltpu.VMEM((2, ROWS, width), F32),
                pltpu.VMEM((2, ROWS, width), F32),
                pltpu.VMEM((2, n_grp - 1, 1, t), F32),
                pltpu.VMEM((2, 1, t), F32),
                pltpu.VMEM((2, n_oct, 1, rows), F32),
                pltpu.VMEM((2, 2, 1, rows), F32),
                pltpu.VMEM((2, 1, rows), F32),
                pltpu.VMEM((n0, 2, rows // 2, width // n0), BF16),
                pltpu.VMEM((n1, 2, rows // 2, width // n1), BF16),
                pltpu.VMEM((n0, n_oct, 2, ROWS, width // n0), BF16),
                pltpu.VMEM((n1, n_oct, 2, ROWS, width // n1), BF16),
                pltpu.VMEM((n0, 2, ROWS, width // n0), BF16),
                pltpu.VMEM((n0, 2, ROWS, width // n0), BF16),
                pltpu.VMEM((n1, ROWS, width // n1), BF16),
                pltpu.VMEM((n1, ROWS, width // n1), BF16),
                pltpu.VMEM((n0, 2, ROWS, width // n0), BF16),
                pltpu.VMEM((n0, 2, rows // 2, width // n0), BF16),
                pltpu.VMEM((1, rows), F32),
                pltpu.VMEM((n_oct, 1, rows), F32),
                pltpu.VMEM((2, n_grp // 2, ROWS, width), BF16),
                dma, dma, dma, dma, dma,
                dma((2,)), dma((2,)), dma((2,)), dma((2,)), dma((2,)), dma((2,)),
                dma((2, max(PIECES))), dma((2, max(PIECES))), dma((n0,)), dma((n0,)), dma((n1,)), dma((n1,)),
                dma((n0,)), dma((n0,)), dma, dma,
                dma((2, n1)), dma((2, n1)), dma, dma, dma((2, n1)), dma((2, n1)),
            ],
            compiler_params=pltpu.CompilerParams(
                collective_id=0, has_side_effects=True, vmem_limit_bytes=24 * 2**20
            ),
            name="kmeans_decode",
        )(x, c, scale, e)

    placed = (P("seq", None), P("grp", None), P(), P(None, "grp"))
    return jax.shard_map(
        per_device, mesh=mesh, in_specs=placed, out_specs=P(None, "seq", "grp"), check_vma=False
    )
```

```python
import functools

import jax
import jax.numpy as jnp
from jax import lax
from jax.experimental import pallas as pl
from jax.experimental.pallas import tpu as pltpu
from jax.sharding import PartitionSpec as P

MESH = pl.DeviceIdType.MESH
XS, ZL = 4, 4
ZH, YS, CORES = 2, 8, 2
ROWS = 16
F32, BF16 = jnp.float32, jnp.bfloat16
PIECES = (4, 2)


def ring(d, n):
    return min(d, n - d)


OCTET = sorted(
    [(z, x) for z in range(2) for x in range(XS) if z or x], key=lambda p: -(p[0] + ring(p[1], XS))
)
NEAR = sorted([(0, y) for y in range(1, YS)], key=lambda p: -ring(p[1], YS))
FAR = sorted([(1, y) for y in range(YS)], key=lambda p: -ring(p[1], YS))
CHIPS = FAR + NEAR


def seq_index(z, x):
    me = lax.axis_index("seq")
    mz, mx = me // XS, me % XS
    pz = ((mz // 2 + z // 2) % 2) * 2 + (mz % 2 + z % 2) % 2
    return pz * XS + (mx + x) % XS


def grp_index(z, y, c):
    me = lax.axis_index("grp")
    mc, my, mz = me % CORES, (me // CORES) % YS, me // (CORES * YS)
    return (((mz + z) % ZH) * YS + (my + y) % YS) * CORES + (mc + c) % CORES


def kernel(
    x_hbm, c_hbm, scale_ref, e_hbm, out_ref,
    x_ref, c_ref, e_ref, own, theirs_c, lse_buf, lse_src, mass_buf, mass_src, pair_mass,
    w_src0, w_src1, w_buf0, w_buf1, pair_src, pair_buf, last_src, last_buf, c_src, c_next, sq_src, sq_buf, fin,
    x_sem, c_sem, e_sem, a_s, a_r,
    lse_s, lse_r, m_s, m_r, n_s, n_r, w_s, w_r, o_s, o_r, l_s, l_r,
    c_s, c_r, q_s, q_r, f_s, f_r, p_s, p_r, h_s, h_r,
):
    tokens, width = x_hbm.shape
    rows = c_hbm.shape[0]
    w_src, w_buf = (w_src0, w_src1), (w_buf0, w_buf1)
    seq = lax.axis_index("seq")
    partner_group = grp_index(0, 0, 1)
    octet = [{"seq": seq_index(z, x), "grp": partner_group} for z, x in OCTET] + [{"grp": partner_group}]
    octet_index = [seq_index(z, x) % 8 for z, x in OCTET] + [seq % 8]
    across = {"seq": seq_index(2, 0)}
    peers_chip = [{"grp": grp_index(z, y, 0)} for z, y in CHIPS]
    peers_other = [{"grp": grp_index(z, y, 1)} for z, y in CHIPS]
    partner = {"grp": partner_group}
    everyone = [p for pair in zip(peers_chip, peers_other) for p in pair] + octet + [across]

    barrier = pltpu.get_barrier_semaphore()
    for p in everyone:
        pl.semaphore_signal(barrier, inc=1, device_id=p, device_id_type=MESH)
    c_copy = pltpu.make_async_copy(c_hbm, c_ref, c_sem)
    c_copy.start()
    x_copy = pltpu.make_async_copy(x_hbm, x_ref, x_sem)
    x_copy.start()
    e_copy = pltpu.make_async_copy(e_hbm, e_ref, e_sem)
    e_copy.start()
    pending = [e_copy.wait]

    def send(src, dst, ssem, rsem, device):
        pltpu.make_async_remote_copy(
            src_ref=src, dst_ref=dst, send_sem=ssem, recv_sem=rsem,
            device_id=device, device_id_type=MESH,
        ).start()

    def drain(ref, sem):
        pltpu.make_async_copy(ref, ref, sem).wait()

    c_copy.wait()
    c0 = c_ref[...]
    half0 = 0.5 * jnp.sum(c0 * c0, axis=1, keepdims=True)
    factor = 2.0 / (scale_ref[0] * jnp.sqrt(jnp.float32(width)))
    x_copy.wait()
    size = [width // n for n in PIECES]
    cuts = [[slice(h * size[i], (h + 1) * size[i]) for h in range(n)] for i, n in enumerate(PIECES)]

    def softmax(i, centres, half):
        dots = sum(
            lax.dot_general(
                centres[h], x_ref[:, cuts[0][h]], (((1,), (1,)), ((), ())), preferred_element_type=F32
            )
            for h in range(PIECES[0])
        )
        logits = factor * (dots - half)
        top = jnp.max(logits, axis=0, keepdims=True)
        weights = jnp.exp(logits - top)
        lse = top + jnp.log(jnp.sum(weights, axis=0, keepdims=True))
        lse_src[i] = lse
        if i == 0:
            pl.semaphore_wait(barrier, len(everyone))
        slot = 0
        for a, b in zip(peers_chip, peers_other):
            for p in (a, b):
                send(lse_src.at[i], lse_buf.at[i, slot], lse_s.at[i], lse_r.at[i], p)
                slot += 1
        send(lse_src.at[i], lse_buf.at[i, slot], lse_s.at[i], lse_r.at[i], partner)
        pending.append(lambda: drain(lse_buf.at[i], lse_s.at[i]))
        if i == 0:
            for q in range(2):
                start = pl.ds(pl.multiple_of(q * (rows // 2) + (seq % 8) * ROWS, ROWS), ROWS)
                send(c_ref.at[start], theirs_c.at[q], a_s, a_r, partner)
            pending.append(lambda: drain(theirs_c, a_s))
        drain(lse_buf.at[i], lse_r.at[i])
        others = lse_buf[i]
        m = jnp.maximum(jnp.max(others, axis=0), lse)
        total = jnp.sum(jnp.exp(others - m[None]), axis=0) + jnp.exp(lse - m)
        full = m + jnp.log(total)
        resp = (weights * jnp.exp(top - full)).astype(BF16)
        return resp

    n_oct = len(octet)
    j, hi = seq % 8, seq // 8
    lane = lax.broadcasted_iota(jnp.int32, (ROWS, rows), 1)
    row = lax.broadcasted_iota(jnp.int32, (ROWS, rows), 0)
    spots = [lane == q * (rows // 2) + j * ROWS + row for q in range(2)]

    def scatter(i, resp):
        for h, cut in enumerate(cuts[i]):
            w = jnp.dot(resp, x_ref[:, cut], preferred_element_type=F32)
            w_src[i][h] = w.astype(BF16).reshape(2, rows // 2, size[i])
            for k in range(n_oct):
                theirs = pl.ds(pl.multiple_of(octet_index[k] * ROWS, ROWS), ROWS)
                send(w_src[i].at[h, :, theirs], w_buf[i].at[h, k], w_s.at[i, h], w_r.at[i, h], octet[k])
            pending.append(lambda h=h: drain(w_buf[i].at[h], w_s.at[i, h]))
            if h == 0:
                mass = lax.dot_general(
                    jnp.ones((16, tokens), BF16), resp, (((1,), (1,)), ((), ())),
                    preferred_element_type=F32,
                )
                mass_src[i, 0] = mass[0:1]
                for k in range(n_oct):
                    send(mass_src.at[i, 0], mass_buf.at[i, k], m_s.at[i], m_r.at[i], octet[k])
                pending.append(lambda: drain(mass_buf.at[i], m_s.at[i]))

    def partial(i, h, side):
        acc = w_buf[i][h, 0, side].astype(F32)
        for k in range(1, n_oct):
            acc = acc + w_buf[i][h, k, side].astype(F32)
        return acc

    def pair_up_mass(i):
        drain(mass_buf.at[i], m_r.at[i])
        mass = jnp.sum(mass_buf[i], axis=0)
        mass_src[i, 1] = mass
        send(mass_src.at[i, 1], pair_mass.at[i], n_s.at[i], n_r.at[i], across)
        pending.append(lambda: drain(pair_mass.at[i], n_s.at[i]))
        return mass

    scatter(0, softmax(0, [c0[:, cut].astype(BF16) for cut in cuts[0]], half0))
    for h in range(PIECES[0]):
        drain(w_buf[0].at[h], w_r.at[0, h])
        for q in range(2):
            pair_src[h, q] = partial(0, h, q).astype(BF16)
        send(pair_src.at[h], pair_buf.at[h], o_s.at[h], o_r.at[h], across)
        pending.append(lambda h=h: drain(pair_buf.at[h], o_s.at[h]))
        if h == 0:
            mass = pair_up_mass(0)
    drain(pair_mass.at[0], n_r.at[0])
    mass = mass + pair_mass[0]
    bottoms = [jnp.sum(jnp.where(s, mass, 0.0), axis=1, keepdims=True) + 1.0 for s in spots]
    halves = [jnp.zeros((ROWS, 1), F32) for _ in range(2)]
    block = pl.ds(pl.multiple_of(j * ROWS, ROWS), ROWS)
    drain(theirs_c, a_r)
    for h, cut in enumerate(cuts[0]):
        drain(pair_buf.at[h], o_r.at[h])
        for q in range(2):
            both = pair_src[h, q].astype(F32) + pair_buf[h, q].astype(F32)
            centre = (both + theirs_c[q, :, cut]) / bottoms[q]
            own[q, :, cut] = centre
            c_src[h, q] = centre.astype(BF16)
            halves[q] += 0.5 * jnp.sum(centre * centre, axis=1, keepdims=True)
        for k in range(n_oct):
            send(c_src.at[h], c_next.at[h, :, block], c_s.at[h], c_r.at[h], octet[k])
        pending.append(lambda h=h: drain(c_next.at[h], c_s.at[h]))
    sq_src[...] = sum(
        jnp.sum(jnp.where(spots[q], halves[q], 0.0), axis=0, keepdims=True) for q in range(2)
    )
    for k in range(n_oct):
        send(sq_src, sq_buf.at[j], q_s, q_r, octet[k])
    pending.append(lambda: drain(sq_buf, q_s))
    for h in range(PIECES[0]):
        drain(c_next.at[h], c_r.at[h])
    drain(sq_buf, q_r)
    line = jnp.sum(sq_buf[...], axis=0)
    diagonal = lax.broadcasted_iota(jnp.int32, (rows, rows), 0) == lax.broadcasted_iota(
        jnp.int32, (rows, rows), 1
    )
    half1 = jnp.sum(jnp.where(diagonal, line, 0.0), axis=1, keepdims=True)

    scatter(1, softmax(1, [c_next[h].reshape(rows, size[0]) for h in range(PIECES[0])], half1))
    kept = []
    for h in range(PIECES[1]):
        drain(w_buf[1].at[h], w_r.at[1, h])
        last_src[h] = partial(1, h, 1 - hi).astype(BF16)
        send(last_src.at[h], last_buf.at[h], l_s.at[h], l_r.at[h], across)
        pending.append(lambda h=h: drain(last_buf.at[h], l_s.at[h]))
        kept.append(partial(1, h, hi))
        if h == 0:
            mass = pair_up_mass(1)
    drain(pair_mass.at[1], n_r.at[1])
    mass = mass + pair_mass[1]
    bottom = jnp.sum(jnp.where(lane == seq * ROWS + row, mass, 0.0), axis=1, keepdims=True) + 1.0

    def summed(h):
        drain(last_buf.at[h], l_r.at[h])
        return kept[h] + last_buf[h].astype(F32)

    near, far = len(NEAR), len(FAR)
    slots = [1 + near + k for k in range(far)] + [1 + k for k in range(near)]
    first, count = (1, 1 + near), (near, far)
    for h, cut in enumerate(cuts[1]):
        fin[1, 0, :, cut] = ((summed(h) + own[hi, :, cut]) / bottom).astype(BF16)
        lanes = pl.ds(cut.start, size[1])
        for k, slot in enumerate(slots):
            g = 1 if k < far else 0
            send(fin.at[1, 0, :, lanes], fin.at[0, slot, :, lanes], f_s.at[g, h], f_r.at[g, h], peers_other[k])
    send(fin.at[1, 0], fin.at[0, 0], p_s, p_r, partner)
    pending.append(lambda: drain(fin.at[0, 0], p_s))

    def part(c, g, h):
        return fin.at[c, pl.ds(first[g], count[g]), :, pl.ds(cuts[1][h].start, size[1])]

    for g in range(2):
        for h in range(PIECES[1]):
            pending.append(lambda g=g, h=h: drain(part(0, g, h), f_s.at[g, h]))
            drain(part(0, g, h), f_r.at[g, h])
            send(part(0, g, h), part(1, g, h), h_s.at[g, h], h_r.at[g, h], partner)
            pending.append(lambda g=g, h=h: drain(part(1, g, h), h_s.at[g, h]))
    pending.pop(0)()
    drain(fin.at[0, 0], p_r)
    me = lax.axis_index("grp")
    mc, my, mz = me % CORES, (me // CORES) % YS, me // (CORES * YS)
    chips = [(0, 0)] + NEAR + FAR

    def place(half, first, count, d):
        for k in range(count):
            z, y = chips[first + k]
            g = (((mz + ZH - z) % ZH) * YS + (my + YS - y) % YS) * CORES + (mc + half) % CORES
            out_ref[g] = d[k * ROWS : (k + 1) * ROWS]

    def decode(half, first, count):
        part = fin[half, first : first + count].reshape(count * ROWS, width)
        d = jnp.dot(part, e_ref[...], preferred_element_type=F32).astype(BF16)
        place(half, first, count, d)

    decode(0, 0, 2 * far)
    for h in range(PIECES[1]):
        drain(part(1, 0, h), h_r.at[0, h])
    decode(1, 0, far)
    d = None
    for h, cut in enumerate(cuts[1]):
        drain(part(1, 1, h), h_r.at[1, h])
        rows_h = fin[1, far : 2 * far, :, cut].reshape(far * ROWS, size[1])
        d_h = jnp.dot(rows_h, e_ref[cut, :], preferred_element_type=F32)
        d = d_h if d is None else d + d_h
    place(1, far, far, d.astype(BF16))

    for wait in pending:
        wait()


def solution(mesh):
    def per_device(x, c, scale, e):
        t, width = x.shape
        rows = c.shape[0]
        cols = e.shape[1]
        n_grp = ZH * YS * CORES
        n_oct = len(OCTET) + 1
        n0, n1 = PIECES
        hbm = pl.BlockSpec(memory_space=pltpu.HBM)
        dma = pltpu.SemaphoreType.DMA
        x, c, e = (pltpu.with_memory_space_constraint(v, pltpu.HBM) for v in (x, c, e))
        return pl.pallas_call(
            kernel,
            out_shape=jax.ShapeDtypeStruct((n_grp, ROWS, cols), BF16),
            in_specs=[hbm, hbm, pl.BlockSpec(memory_space=pltpu.SMEM), hbm],
            out_specs=pl.BlockSpec(memory_space=pltpu.VMEM),
            scratch_shapes=[
                pltpu.VMEM((t, width), BF16),
                pltpu.VMEM((rows, width), F32),
                pltpu.VMEM((width, cols), BF16),
                pltpu.VMEM((2, ROWS, width), F32),
                pltpu.VMEM((2, ROWS, width), F32),
                pltpu.VMEM((2, n_grp - 1, 1, t), F32),
                pltpu.VMEM((2, 1, t), F32),
                pltpu.VMEM((2, n_oct, 1, rows), F32),
                pltpu.VMEM((2, 2, 1, rows), F32),
                pltpu.VMEM((2, 1, rows), F32),
                pltpu.VMEM((n0, 2, rows // 2, width // n0), BF16),
                pltpu.VMEM((n1, 2, rows // 2, width // n1), BF16),
                pltpu.VMEM((n0, n_oct, 2, ROWS, width // n0), BF16),
                pltpu.VMEM((n1, n_oct, 2, ROWS, width // n1), BF16),
                pltpu.VMEM((n0, 2, ROWS, width // n0), BF16),
                pltpu.VMEM((n0, 2, ROWS, width // n0), BF16),
                pltpu.VMEM((n1, ROWS, width // n1), BF16),
                pltpu.VMEM((n1, ROWS, width // n1), BF16),
                pltpu.VMEM((n0, 2, ROWS, width // n0), BF16),
                pltpu.VMEM((n0, 2, rows // 2, width // n0), BF16),
                pltpu.VMEM((1, rows), F32),
                pltpu.VMEM((n_oct, 1, rows), F32),
                pltpu.VMEM((2, n_grp // 2, ROWS, width), BF16),
                dma, dma, dma, dma, dma,
                dma((2,)), dma((2,)), dma((2,)), dma((2,)), dma((2,)), dma((2,)),
                dma((2, max(PIECES))), dma((2, max(PIECES))), dma((n0,)), dma((n0,)), dma((n1,)), dma((n1,)),
                dma((n0,)), dma((n0,)), dma, dma,
                dma((2, n1)), dma((2, n1)), dma, dma, dma((2, n1)), dma((2, n1)),
            ],
            compiler_params=pltpu.CompilerParams(
                collective_id=0, has_side_effects=True, vmem_limit_bytes=24 * 2**20
            ),
            name="kmeans_decode",
        )(x, c, scale, e)

    placed = (P("seq", None), P("grp", None), P(), P(None, "grp"))
    return jax.shard_map(
        per_device, mesh=mesh, in_specs=placed, out_specs=P(None, "seq", "grp"), check_vma=False
    )
```
